32 devices in a mesh: pix: 8 (over z, x), feat: 4 (over y, core).
Axes of the slice: x: 2, y: 2, z: 4, core: 2. Of those that a mesh axis runs over, the one named last changes fastest.
Arguments:
- mass_bin: int32 [32768, 256], P(('pix', 'feat')), may hold values from 0 to 255
- mobility_bin: int32 [32768, 256], P(('pix', 'feat')), may hold values from 0 to 15
- intensity: bfloat16 [32768, 256], P(('pix', 'feat')), may hold values from 10 to 4000, as said below
- basis_init: float32 [32768, 64], P(('pix', 'feat')), may hold values from 0.1 to 1
- profile_init: float32 [64, 4096], P(None, 'feat'), may hold values from 0.1 to 1
Outputs:
- basis: float32 [32768, 64], P(('pix', 'feat'))
- profiles: float32 [64, 4096], P(None, 'feat')
The draws below stay inside these ranges and needn't reach their ends.
Inputs may be any that keep to these rules, and one draw needn't show every extreme that they name: `intensity`: positive peak intensities.
All inputs are finite; a program needn't handle non-finite values.
Results may differ from the reference program's by a relative error of at most 0.00045.
Values may be sent and summed in bfloat16 or wider, within the bound.
A program may use at most 64 MiB of HBM per device.

```python
import math
import jax
import jax.numpy as jnp
from jax import lax

MZ = 256
MOB = 16
RANK = 64
PEAKS = 256
ITERS = 2
FEATS = 4096
PIXELS = 32768


def draw_intensity(key, part):
    rows = jnp.arange(PIXELS, dtype=jnp.float32)[:, None] / PIXELS
    scale = 0.3 * jnp.exp(rows * jnp.log(10.0))
    values = jnp.exp(jax.random.uniform(key, (PIXELS, PEAKS), jnp.float32, jnp.log(50.0), jnp.log(1000.0)))
    return (values * scale).astype(jnp.bfloat16)


def plant(array, own_key, least, high):
    longest = array.shape.index(max(array.shape))
    spots = []
    for shift in (0, 1):
        where = [jax.random.randint(jax.random.fold_in(own_key, axis), (), 0, length) for axis, length in enumerate(array.shape)]
        where[longest] = (where[longest] + shift) % array.shape[longest]
        spots.append(tuple(where))
    return array.at[spots[0]].set(least).at[spots[1]].set(high)


def shard_levels(stream_key, shape, cuts, least, top_value):
    loudness, own = 1.0, jax.random.fold_in(stream_key, 6)
    for dim, parts in cuts:
        heights = jnp.exp(jax.random.uniform(jax.random.fold_in(own, dim), (parts,), jnp.float32, least / len(cuts), top_value / len(cuts)))
        loudness = loudness * jnp.repeat(heights, shape[dim] // parts).reshape([-1 if axis == dim else 1 for axis in range(len(shape))])
    return loudness


def setup_inputs(seed: int = 0) -> dict:
    splits = jax.random.split(jax.random.key(seed), 6)
    mass_bin = plant(jax.random.randint(splits[0], (PIXELS, PEAKS), 0, MZ), jax.random.fold_in(splits[0], 1), 0, MZ - 1).astype(jnp.int32)
    mobility_bin = plant(jax.random.randint(splits[1], (PIXELS, PEAKS), 0, MOB), jax.random.fold_in(splits[1], 1), 0, MOB - 1).astype(jnp.int32)
    intensity = draw_intensity(jax.random.fold_in(splits[5], 71), 0)
    basis_init = jnp.clip(0.1 + 0.9 * jax.random.uniform(splits[3], (PIXELS, RANK), jnp.float32) ** shard_levels(splits[3], (PIXELS, RANK), ((0, 32),), -0.2, 0.2), 0.1, 1.0)
    profile_init = jnp.clip(0.1 + 0.9 * jax.random.uniform(splits[4], (RANK, FEATS), jnp.float32) ** shard_levels(splits[4], (RANK, FEATS), ((1, 4),), -0.2, 0.2), 0.1, 1.0)
    return dict(mass_bin=mass_bin, mobility_bin=mobility_bin, intensity=intensity, basis_init=basis_init, profile_init=profile_init)


EPS = 1e-6


def bin_block(args):
    mass, mobility, weight = args
    feature = (mobility * MZ + mass).astype(jnp.int32)
    rows = jnp.broadcast_to(jnp.arange(mass.shape[0], dtype=jnp.int32)[:, None], mass.shape)
    dense = jnp.zeros((mass.shape[0], MZ * MOB), jnp.float32)
    dense = dense.at[rows, feature].add(weight.astype(jnp.float32))
    return dense.astype(jnp.bfloat16)


def reference(mass_bin, mobility_bin, intensity, basis_init, profile_init):
    block = math.gcd(PIXELS, 4096)
    count = PIXELS // block
    spectra = lax.map(bin_block, (mass_bin.reshape(count, block, PEAKS), mobility_bin.reshape(count, block, PEAKS), intensity.reshape(count, block, PEAKS)))
    spectra = spectra.reshape(PIXELS, MZ * MOB)
    basis, profiles = basis_init, profile_init
    highest = lax.Precision.HIGHEST
    for step in range(ITERS):
        numer_h = lax.dot_general(basis.astype(jnp.bfloat16), spectra, (((0,), (0,)), ((), ())), preferred_element_type=jnp.float32)
        gram_w = lax.dot_general(basis, basis, (((0,), (0,)), ((), ())), precision=highest, preferred_element_type=jnp.float32)
        profiles = profiles * numer_h / (jnp.dot(gram_w, profiles, precision=highest, preferred_element_type=jnp.float32) + EPS)
        numer_w = lax.dot_general(spectra, profiles.astype(jnp.bfloat16), (((1,), (1,)), ((), ())), preferred_element_type=jnp.float32)
        gram_h = lax.dot_general(profiles, profiles, (((1,), (1,)), ((), ())), precision=highest, preferred_element_type=jnp.float32)
        basis = basis * numer_w / (jnp.dot(basis, gram_h, precision=highest, preferred_element_type=jnp.float32) + EPS)
    return basis, profiles
```

```python
import jax
import jax.numpy as jnp
from jax import lax
from jax.experimental import pallas as pl
from jax.experimental.pallas import tpu as pltpu
from jax.sharding import PartitionSpec as P

LANES = 128
MZ = 256
MOB = 16
HI = MZ * MOB // LANES
GROUP = 16
ITERS = 2
EPS = 1e-06


def bin_kernel(mass_ref, mobility_ref, weight_ref, out_ref, hi_ref, lo_ref, value_ref, dense_ref):
    rows, peaks = mass_ref.shape
    mass = mass_ref[...]
    hi_ref[...] = (mobility_ref[...] * (MZ // LANES) + mass // LANES).astype(jnp.float32)
    lo_ref[...] = (mass % LANES).astype(jnp.float32)
    value_ref[...] = weight_ref[...].astype(jnp.float32)
    hi_iota = lax.broadcasted_iota(jnp.int32, (HI, peaks), 0).astype(jnp.float32).astype(jnp.bfloat16)
    lo_iota = lax.broadcasted_iota(jnp.int32, (LANES, peaks), 0).astype(jnp.float32).astype(jnp.bfloat16)

    def spread(ref, p, count):
        return jnp.broadcast_to(ref[pl.ds(p, 1), :], (count, peaks)).astype(jnp.bfloat16)

    def group(g, _):
        base = pl.multiple_of(g * GROUP, GROUP)
        for i in range(GROUP):
            p = base + i
            left = jnp.where(
                spread(hi_ref, p, HI) == hi_iota, spread(value_ref, p, HI), jnp.bfloat16(0)
            )
            right = jnp.where(
                spread(lo_ref, p, LANES) == lo_iota, jnp.bfloat16(1), jnp.bfloat16(0)
            )
            dense_ref[pl.ds(i, HI, stride=GROUP), :] = lax.dot_general(
                left, right, (((1,), (1,)), ((), ())), preferred_element_type=jnp.float32
            )
        for h in range(HI):
            out_ref[pl.ds(base, GROUP), h * LANES : (h + 1) * LANES] = dense_ref[
                h * GROUP : (h + 1) * GROUP, :
            ].astype(jnp.bfloat16)
        return 0

    lax.fori_loop(0, rows // GROUP, group, 0)


def bin_peaks(mass, mobility, weight):
    rows, peaks = mass.shape
    block = 128
    spec = pl.BlockSpec((block, peaks), lambda i: (i, 0))
    return pl.pallas_call(
        bin_kernel,
        out_shape=jax.ShapeDtypeStruct((rows, MZ * MOB), jnp.bfloat16),
        grid=(rows // block,),
        in_specs=[spec] * 3,
        out_specs=pl.BlockSpec((block, MZ * MOB), lambda i: (i, 0)),
        scratch_shapes=[pltpu.VMEM((block, peaks), jnp.float32)] * 3
        + [pltpu.VMEM((HI * GROUP, LANES), jnp.float32)],
        cost_estimate=pl.CostEstimate(
            flops=2 * rows * peaks * MZ * MOB, bytes_accessed=rows * (peaks * 10 + MZ * MOB * 2), transcendentals=0
        ),
    )(mass, mobility, weight)


def local(mass_bin, mobility_bin, intensity, basis_init, profile_init):
    spectra = bin_peaks(mass_bin, mobility_bin, intensity)
    highest = lax.Precision.HIGHEST
    basis, profiles = (basis_init, profile_init)
    for step in range(ITERS):
        partial_h = lax.dot_general(
            basis.astype(jnp.bfloat16),
            spectra,
            (((0,), (0,)), ((), ())),
            preferred_element_type=jnp.float32,
        )
        partial_gram = lax.dot_general(
            basis,
            basis,
            (((0,), (0,)), ((), ())),
            precision=highest,
            preferred_element_type=jnp.float32,
        )
        shared = lax.psum_scatter(partial_h, "feat", scatter_dimension=1, tiled=True)
        numer_h = lax.psum(shared, "pix")
        gram_w = lax.psum(partial_gram, ("pix", "feat"))
        profiles = (
            profiles
            * numer_h
            / (
                jnp.dot(gram_w, profiles, precision=highest, preferred_element_type=jnp.float32)
                + EPS
            )
        )
        numer_w = lax.dot_general(
            spectra,
            lax.all_gather(profiles.astype(jnp.bfloat16), "feat", axis=1, tiled=True),
            (((1,), (1,)), ((), ())),
            preferred_element_type=jnp.float32,
        )
        local_gram = lax.dot_general(
            profiles,
            profiles,
            (((1,), (1,)), ((), ())),
            precision=highest,
            preferred_element_type=jnp.float32,
        )
        gram_h = lax.psum(local_gram, "feat")
        basis = (
            basis
            * numer_w
            / (jnp.dot(basis, gram_h, precision=highest, preferred_element_type=jnp.float32) + EPS)
        )
    return (basis, profiles)


def solution(mesh):
    return jax.shard_map(
        local,
        mesh=mesh,
        in_specs=(
            P(("pix", "feat"), None),
            P(("pix", "feat"), None),
            P(("pix", "feat"), None),
            P(("pix", "feat"), None),
            P(None, "feat"),
        ),
        out_specs=(P(("pix", "feat"), None), P(None, "feat")),
        check_vma=False,
    )
```

```python
import functools

import jax
import jax.numpy as jnp
from jax import lax
from jax.experimental import pallas as pl
from jax.experimental.pallas import tpu as pltpu
from jax.sharding import PartitionSpec as P

LANES = 128
MZ = 256
MOB = 16
HI = MZ * MOB // LANES
GROUP = 16
ITERS = 2
EPS = 1e-06


def bin_kernel(mass_ref, mobility_ref, weight_ref, out_ref, hi_ref, lo_ref, value_ref, dense_ref):
    rows, peaks = mass_ref.shape
    mass = mass_ref[...]
    hi_ref[...] = (mobility_ref[...] * (MZ // LANES) + mass // LANES).astype(jnp.float32)
    lo_ref[...] = (mass % LANES).astype(jnp.float32)
    value_ref[...] = weight_ref[...].astype(jnp.float32)
    hi_iota = lax.broadcasted_iota(jnp.int32, (HI, peaks), 0).astype(jnp.float32).astype(jnp.bfloat16)
    lo_iota = lax.broadcasted_iota(jnp.int32, (LANES, peaks), 0).astype(jnp.float32).astype(jnp.bfloat16)

    def spread(ref, p, count):
        return jnp.broadcast_to(ref[pl.ds(p, 1), :], (count, peaks)).astype(jnp.bfloat16)

    def group(g, _):
        base = pl.multiple_of(g * GROUP, GROUP)
        for i in range(GROUP):
            p = base + i
            left = jnp.where(
                spread(hi_ref, p, HI) == hi_iota, spread(value_ref, p, HI), jnp.bfloat16(0)
            )
            right = jnp.where(
                spread(lo_ref, p, LANES) == lo_iota, jnp.bfloat16(1), jnp.bfloat16(0)
            )
            dense_ref[pl.ds(i, HI, stride=GROUP), :] = lax.dot_general(
                left, right, (((1,), (1,)), ((), ())), preferred_element_type=jnp.float32
            )
        for h in range(HI):
            out_ref[pl.ds(base, GROUP), h * LANES : (h + 1) * LANES] = dense_ref[
                h * GROUP : (h + 1) * GROUP, :
            ].astype(jnp.bfloat16)
        return 0

    lax.fori_loop(0, rows // GROUP, group, 0)


def bin_peaks(mass, mobility, weight):
    rows, peaks = mass.shape
    block = 128
    spec = pl.BlockSpec((block, peaks), lambda i: (i, 0))
    return pl.pallas_call(
        bin_kernel,
        out_shape=jax.ShapeDtypeStruct((rows, MZ * MOB), jnp.bfloat16),
        grid=(rows // block,),
        in_specs=[spec] * 3,
        out_specs=pl.BlockSpec((block, MZ * MOB), lambda i: (i, 0)),
        scratch_shapes=[pltpu.VMEM((block, peaks), jnp.float32)] * 3
        + [pltpu.VMEM((HI * GROUP, LANES), jnp.float32)],
        cost_estimate=pl.CostEstimate(
            flops=2 * rows * peaks * MZ * MOB, bytes_accessed=rows * (peaks * 10 + MZ * MOB * 2), transcendentals=0
        ),
    )(mass, mobility, weight)


def nmf_kernel(
    pixes, chips, spectra_ref, basis_in, profiles_in, basis_ref, profiles_ref,
    pair_out, pair_in, gram_out, gram_in, chip_out, chip_in, pix_out, pix_in, whole_ref,
    rounded_ref, gram_h_out, gram_h_in, gram_h_pair_out, gram_h_pair_in, padded_ref,
    pair_sem, gram_sem, chip_sem, pix_sem, whole_sem, block_sem, block_pair_sem, gram_h_sem, gram_h_pair_sem,
):
    rank, width = profiles_in.shape
    share = rank // pixes
    pix, feat = lax.axis_index("pix"), lax.axis_index("feat")
    core, chip = lax.rem(feat, 2), feat // 2
    other = 1 - core
    partner = (pix, chip * 2 + other)
    highest = lax.Precision.HIGHEST

    def chip_at(j):
        return lax.rem(chip + j + chips, chips)

    def pix_at(d):
        return lax.rem(pix + d + pixes, pixes)

    barrier = pltpu.get_barrier_semaphore()
    peers = [partner] + [(pix, chip_at(j) * 2 + core) for j in range(1, chips)]
    peers += [(pix_at(d), feat) for d in range(1, pixes)]
    for peer in peers:
        pl.semaphore_signal(barrier, inc=1, device_id=peer, device_id_type=pl.DeviceIdType.MESH)
    pl.semaphore_wait(barrier, len(peers))

    started = []

    def send(src, dst, sems, device):
        copy = pltpu.make_async_remote_copy(
            src_ref=src, dst_ref=dst, send_sem=sems.at[0], recv_sem=sems.at[1],
            device_id=device, device_id_type=pl.DeviceIdType.MESH,
        )
        copy.start()
        started.append(copy)
        return copy

    def columns(block):
        return pl.ds(pl.multiple_of(block * width, LANES), width)

    padded_ref[...] = jnp.zeros_like(padded_ref)
    gram_h_out[...] = jnp.zeros_like(gram_h_out)
    basis, profiles = basis_in[...], profiles_in[...]
    for step in range(ITERS):
        padded_ref[:, :rank] = basis
        padded = padded_ref[...]
        turned = padded.T[:rank, :]
        turned_b = turned.astype(jnp.bfloat16)

        def numer(block):
            return jnp.dot(
                turned_b, spectra_ref[:, columns(block)], preferred_element_type=jnp.float32
            )

        order = list(range(1, chips)) + [0]
        pair = {}
        for j in order:
            pair_out[step, j] = numer(chip_at(j) * 2 + other)
            pair[j] = send(pair_out.at[step, j], pair_in.at[step, j], pair_sem.at[step, j], partner)
        gram_out[step] = jnp.dot(turned, padded, precision=highest, preferred_element_type=jnp.float32)
        gram_copy = send(gram_out.at[step], gram_in.at[step], gram_sem.at[step], partner)
        chip_copy = {}
        for j in order:
            mine = numer(chip_at(j) * 2 + core)
            if j == order[0]:
                gram_copy.wait_recv()
                gram = gram_out[step] + gram_in[step]
            pair[j].wait_recv()
            chip_out[step, j, :, :width] = mine + pair_in[step, j]
            chip_out[step, j, :, width:] = gram
            if j:
                chip_copy[j] = send(
                    chip_out.at[step, j], chip_in.at[step, j], chip_sem.at[step, j], (pix, chip_at(j) * 2 + core)
                )
        total = chip_out[step, 0]
        for j in range(1, chips):
            chip_copy[j].wait_recv()
            total = total + chip_in[step, j]
        if share % 8 == 0:
            pix_out[step] = total.reshape(pixes, share, width + LANES)
        else:
            for d in range(pixes):
                pix_out[step, d] = total[d * share : (d + 1) * share]
        copies = [
            send(pix_out.at[step, pix_at(d)], pix_in.at[step, d], pix_sem.at[step, d], (pix_at(d), feat))
            for d in range(1, pixes)
        ]
        part = pix_out[step, pix]
        for d in range(1, pixes):
            copies[d - 1].wait_recv()
            part = part + pix_in[step, d]
        whole_ref[step, pix] = part
        copies = [
            send(whole_ref.at[step, pix], whole_ref.at[step, pix], whole_sem.at[step, d], (pix_at(d), feat))
            for d in range(1, pixes)
        ]
        for copy in copies:
            copy.wait_recv()
        if share % 8 == 0:
            whole = whole_ref[step].reshape(rank, width + LANES)
        else:
            for d in range(pixes):
                chip_out[step, 0, d * share : (d + 1) * share] = whole_ref[step, d]
            whole = chip_out[step, 0]
        gram_w = whole[:, width : width + rank]
        profiles = (
            profiles
            * whole[:, :width]
            / (jnp.dot(gram_w, profiles, precision=highest, preferred_element_type=jnp.float32) + EPS)
        )
        rounded_ref[step, feat] = profiles.astype(jnp.bfloat16)
        mine = rounded_ref.at[step, feat]
        block_copy = {
            j: send(mine, mine, block_sem.at[step, j], (pix, chip_at(j) * 2 + core)) for j in range(1, chips)
        }
        block_pair = {0: send(mine, mine, block_pair_sem.at[step, 0], partner)}
        gram_h_out[step, :, :rank] = lax.dot_general(
            profiles, profiles, (((1,), (1,)), ((), ())), precision=highest, preferred_element_type=jnp.float32
        )
        gram_h_copy = {
            j: send(gram_h_out.at[step], gram_h_in.at[step, j], gram_h_sem.at[step, j], (pix, chip_at(j) * 2 + core))
            for j in range(1, chips)
        }

        def weigh(block):
            return lax.dot_general(
                spectra_ref[:, columns(block)],
                rounded_ref[step, block],
                (((1,), (1,)), ((), ())),
                preferred_element_type=jnp.float32,
            )

        numer_w = weigh(feat)
        gram_h = gram_h_out[step]
        for j in range(1, chips):
            block_copy[j].wait_recv()
            came = rounded_ref.at[step, chip_at(-j) * 2 + core]
            block_pair[j] = send(came, came, block_pair_sem.at[step, j], partner)
            gram_h_copy[j].wait_recv()
            gram_h = gram_h + gram_h_in[step, j]
        gram_h_pair_out[step] = gram_h
        gram_h_pair = send(
            gram_h_pair_out.at[step], gram_h_pair_in.at[step], gram_h_pair_sem.at[step], partner
        )
        for j in range(1, chips):
            numer_w = numer_w + weigh(chip_at(-j) * 2 + core)
        for j in range(chips):
            block_pair[j].wait_recv()
            numer_w = numer_w + weigh(chip_at(-j) * 2 + other)
        gram_h_pair.wait_recv()
        gram_h = (gram_h + gram_h_pair_in[step])[:, :rank]
        basis = (
            basis
            * numer_w
            / (jnp.dot(basis, gram_h, precision=highest, preferred_element_type=jnp.float32) + EPS)
        )
    basis_ref[...] = basis
    profiles_ref[...] = profiles
    for copy in started:
        copy.wait_send()


def nmf(pixes, feats, spectra, basis, profiles):
    rank, width = profiles.shape
    rows = basis.shape[0]
    chips, share = feats // 2, rank // pixes
    f32 = jnp.float32
    dma = pltpu.SemaphoreType.DMA
    return pl.pallas_call(
        functools.partial(nmf_kernel, pixes, chips),
        out_shape=[jax.ShapeDtypeStruct(basis.shape, f32), jax.ShapeDtypeStruct(profiles.shape, f32)],
        in_specs=[pl.BlockSpec(memory_space=pltpu.VMEM)] * 3,
        out_specs=[pl.BlockSpec(memory_space=pltpu.VMEM)] * 2,
        scratch_shapes=[
            pltpu.VMEM((ITERS, chips, rank, width), f32),
            pltpu.VMEM((ITERS, chips, rank, width), f32),
            pltpu.VMEM((ITERS, rank, LANES), f32),
            pltpu.VMEM((ITERS, rank, LANES), f32),
            pltpu.VMEM((ITERS, chips, rank, width + LANES), f32),
            pltpu.VMEM((ITERS, chips, rank, width + LANES), f32),
            pltpu.VMEM((ITERS, pixes, share, width + LANES), f32),
            pltpu.VMEM((ITERS, pixes, share, width + LANES), f32),
            pltpu.VMEM((ITERS, pixes, share, width + LANES), f32),
            pltpu.VMEM((ITERS, feats, rank, width), jnp.bfloat16),
            pltpu.VMEM((ITERS, rank, LANES), f32),
            pltpu.VMEM((ITERS, chips, rank, LANES), f32),
            pltpu.VMEM((ITERS, rank, LANES), f32),
            pltpu.VMEM((ITERS, rank, LANES), f32),
            pltpu.VMEM((rows, LANES), f32),
            dma((ITERS, chips, 2)),
            dma((ITERS, 2)),
            dma((ITERS, chips, 2)),
            dma((ITERS, pixes, 2)),
            dma((ITERS, pixes, 2)),
            dma((ITERS, chips, 2)),
            dma((ITERS, chips, 2)),
            dma((ITERS, chips, 2)),
            dma((ITERS, 2)),
        ],
        compiler_params=pltpu.CompilerParams(
            collective_id=0, has_side_effects=True, vmem_limit_bytes=44 * 1024 * 1024
        ),
    )(spectra, basis, profiles)


def solution(mesh):
    pixes, feats = mesh.shape["pix"], mesh.shape["feat"]

    def local(mass_bin, mobility_bin, intensity, basis_init, profile_init):
        spectra = bin_peaks(mass_bin, mobility_bin, intensity)
        return tuple(nmf(pixes, feats, spectra, basis_init, profile_init))

    return jax.shard_map(
        local,
        mesh=mesh,
        in_specs=(
            P(("pix", "feat"), None),
            P(("pix", "feat"), None),
            P(("pix", "feat"), None),
            P(("pix", "feat"), None),
            P(None, "feat"),
        ),
        out_specs=(P(("pix", "feat"), None), P(None, "feat")),
        check_vma=False,
    )
```

```python
import functools

import jax
import jax.numpy as jnp
from jax import lax
from jax.experimental import pallas as pl
from jax.experimental.pallas import tpu as pltpu
from jax.sharding import PartitionSpec as P

LANES = 128
MZ = 256
MOB = 16
HI = MZ * MOB // LANES
GROUP = 16
ITERS = 2
HALVES = 2
EPS = 1e-06


def bin_kernel(mass_ref, mobility_ref, weight_ref, out_ref, hi_ref, lo_ref, value_ref, dense_ref):
    rows, peaks = mass_ref.shape
    mass = mass_ref[...]
    hi_ref[...] = (mobility_ref[...] * (MZ // LANES) + mass // LANES).astype(jnp.float32)
    lo_ref[...] = (mass % LANES).astype(jnp.float32)
    value_ref[...] = weight_ref[...].astype(jnp.float32)
    hi_iota = lax.broadcasted_iota(jnp.int32, (HI, peaks), 0).astype(jnp.float32).astype(jnp.bfloat16)
    lo_iota = lax.broadcasted_iota(jnp.int32, (LANES, peaks), 0).astype(jnp.float32).astype(jnp.bfloat16)

    def spread(ref, p, count):
        return jnp.broadcast_to(ref[pl.ds(p, 1), :], (count, peaks)).astype(jnp.bfloat16)

    def group(g, _):
        base = pl.multiple_of(g * GROUP, GROUP)
        for i in range(GROUP):
            p = base + i
            left = jnp.where(
                spread(hi_ref, p, HI) == hi_iota, spread(value_ref, p, HI), jnp.bfloat16(0)
            )
            right = jnp.where(
                spread(lo_ref, p, LANES) == lo_iota, jnp.bfloat16(1), jnp.bfloat16(0)
            )
            dense_ref[pl.ds(i, HI, stride=GROUP), :] = lax.dot_general(
                left, right, (((1,), (1,)), ((), ())), preferred_element_type=jnp.float32
            )
        for h in range(HI):
            out_ref[pl.ds(base, GROUP), h * LANES : (h + 1) * LANES] = dense_ref[
                h * GROUP : (h + 1) * GROUP, :
            ].astype(jnp.bfloat16)
        return 0

    lax.fori_loop(0, rows // GROUP, group, 0)


def bin_peaks(mass, mobility, weight):
    rows, peaks = mass.shape
    block = 128
    spec = pl.BlockSpec((block, peaks), lambda i: (i, 0))
    return pl.pallas_call(
        bin_kernel,
        out_shape=jax.ShapeDtypeStruct((rows, MZ * MOB), jnp.bfloat16),
        grid=(rows // block,),
        in_specs=[spec] * 3,
        out_specs=pl.BlockSpec((block, MZ * MOB), lambda i: (i, 0)),
        scratch_shapes=[pltpu.VMEM((block, peaks), jnp.float32)] * 3
        + [pltpu.VMEM((HI * GROUP, LANES), jnp.float32)],
        cost_estimate=pl.CostEstimate(
            flops=2 * rows * peaks * MZ * MOB, bytes_accessed=rows * (peaks * 10 + MZ * MOB * 2), transcendentals=0
        ),
    )(mass, mobility, weight)


def nmf_kernel(
    pixes, chips, spectra_ref, basis_in, profiles_in, basis_ref, profiles_ref,
    pair_out, pair_in, gram_out, gram_in, chip_out, chip_in, pix_out, pix_in, whole_ref,
    rounded_ref, gram_h_out, gram_h_in, gram_h_pair_out, gram_h_pair_in, padded_ref,
    pair_sem, gram_sem, chip_sem, pix_sem, whole_sem, block_sem, block_pair_sem, gram_h_sem, gram_h_pair_sem,
):
    rank, width = profiles_in.shape
    span = width // HALVES
    share = rank // pixes
    pix, feat = lax.axis_index("pix"), lax.axis_index("feat")
    core, chip = lax.rem(feat, 2), feat // 2
    other = 1 - core
    partner = (pix, chip * 2 + other)
    highest = lax.Precision.HIGHEST

    def chip_at(j):
        return lax.rem(chip + j + chips, chips)

    def pix_at(d):
        return lax.rem(pix + d + pixes, pixes)

    barrier = pltpu.get_barrier_semaphore()
    peers = [partner] + [(pix, chip_at(j) * 2 + core) for j in range(1, chips)]
    peers += [(pix_at(d), feat) for d in range(1, pixes)]
    for peer in peers:
        pl.semaphore_signal(barrier, inc=1, device_id=peer, device_id_type=pl.DeviceIdType.MESH)
    pl.semaphore_wait(barrier, len(peers))

    started = []

    def send(src, dst, sems, device):
        copy = pltpu.make_async_remote_copy(
            src_ref=src, dst_ref=dst, send_sem=sems.at[0], recv_sem=sems.at[1],
            device_id=device, device_id_type=pl.DeviceIdType.MESH,
        )
        copy.start()
        started.append(copy)
        return copy

    def columns(block, half):
        return pl.ds(pl.multiple_of(block * width + half * span, LANES), span)

    def reach(half):
        return pl.ds(0, span if half else span + LANES)

    gram_out[...] = jnp.zeros_like(gram_out)
    gram_h_out[...] = jnp.zeros_like(gram_h_out)
    padded_ref[...] = jnp.zeros_like(padded_ref)
    basis = basis_in[...]
    profiles = [profiles_in[:, half * span : (half + 1) * span] for half in range(HALVES)]
    order = list(range(1, chips)) + [0]
    nt = (((1,), (1,)), ((), ()))
    for step in range(ITERS):
        basis_b = basis.astype(jnp.bfloat16)

        def numer(block, half):
            return jnp.dot(
                basis_b, spectra_ref[:, columns(block, half)], preferred_element_type=jnp.float32
            )

        pair, chip_copy, pix_copy, whole_copy, block_copy, block_pair = {}, {}, {}, {}, {}, {}
        for half in range(HALVES):
            for j in order:
                pair_out[step, half, j] = numer(chip_at(j) * 2 + other, half)
                pair[half, j] = send(
                    pair_out.at[step, half, j], pair_in.at[step, half, j], pair_sem.at[step, half, j], partner
                )
            if half == 0:
                gram_out[step, :, :rank] = lax.dot_general(
                    basis, basis, nt, precision=highest, preferred_element_type=jnp.float32
                )
                gram_copy = send(gram_out.at[step], gram_in.at[step], gram_sem.at[step], partner)
            for j in order:
                mine = numer(chip_at(j) * 2 + core, half)
                if half == 0 and j == order[0]:
                    gram_copy.wait_recv()
                    gram = gram_out[step] + gram_in[step]
                pair[half, j].wait_recv()
                chip_out[step, half, j, :, :span] = mine + pair_in[step, half, j]
                if half == 0:
                    chip_out[step, half, j, :, span:] = gram
                if j:
                    chip_copy[half, j] = send(
                        chip_out.at[step, half, j, :, reach(half)],
                        chip_in.at[step, half, j, :, reach(half)],
                        chip_sem.at[step, half, j],
                        (pix, chip_at(j) * 2 + core),
                    )
        for half in range(HALVES):
            size = span if half else span + LANES
            total = chip_out[step, half, 0, :, :size]
            for j in range(1, chips):
                chip_copy[half, j].wait_recv()
                total = total + chip_in[step, half, j, :, :size]
            if share % 8 == 0:
                pix_out[step, half, :, :, :size] = total.reshape(pixes, share, size)
            else:
                for d in range(pixes):
                    pix_out[step, half, d, :, :size] = total[d * share : (d + 1) * share]
            for d in range(1, pixes):
                pix_copy[half, d] = send(
                    pix_out.at[step, half, pix_at(d), :, reach(half)],
                    pix_in.at[step, half, d, :, reach(half)],
                    pix_sem.at[step, half, d],
                    (pix_at(d), feat),
                )
        for half in range(HALVES):
            size = span if half else span + LANES
            part = pix_out[step, half, pix, :, :size]
            for d in range(1, pixes):
                pix_copy[half, d].wait_recv()
                part = part + pix_in[step, half, d, :, :size]
            whole_ref[step, half, pix, :, :size] = part
            for d in range(1, pixes):
                own = whole_ref.at[step, half, pix, :, reach(half)]
                whole_copy[half, d] = send(own, own, whole_sem.at[step, half, d], (pix_at(d), feat))
        for half in range(HALVES):
            size = span if half else span + LANES
            for d in range(1, pixes):
                whole_copy[half, d].wait_recv()
            if share % 8 == 0:
                whole = whole_ref[step, half, :, :, :size].reshape(rank, size)
            else:
                for d in range(pixes):
                    chip_out[step, half, 0, d * share : (d + 1) * share, :size] = whole_ref[step, half, d, :, :size]
                whole = chip_out[step, half, 0, :, :size]
            if half == 0:
                gram_w = whole[:, span : span + rank]
            profiles[half] = (
                profiles[half]
                * whole[:, :span]
                / (jnp.dot(gram_w, profiles[half], precision=highest, preferred_element_type=jnp.float32) + EPS)
            )
            rounded_ref[step, half, feat] = profiles[half].astype(jnp.bfloat16)
            mine = rounded_ref.at[step, half, feat]
            for j in range(1, chips):
                block_copy[half, j] = send(
                    mine, mine, block_sem.at[step, half, j], (pix, chip_at(j) * 2 + core)
                )
            block_pair[half, 0] = send(mine, mine, block_pair_sem.at[step, half, 0], partner)
            part = lax.dot_general(
                profiles[half], profiles[half], nt, precision=highest, preferred_element_type=jnp.float32
            )
            gram_h = gram_h + part if half else part
        gram_h_out[step, :, :rank] = gram_h
        gram_h_copy = {
            j: send(gram_h_out.at[step], gram_h_in.at[step, j], gram_h_sem.at[step, j], (pix, chip_at(j) * 2 + core))
            for j in range(1, chips)
        }

        def weigh(block, half):
            return lax.dot_general(
                spectra_ref[:, columns(block, half)],
                rounded_ref[step, half, block],
                nt,
                preferred_element_type=jnp.float32,
            )

        numer_w = weigh(feat, 0)
        for half in range(1, HALVES):
            numer_w = numer_w + weigh(feat, half)
        for half in range(HALVES):
            block_pair[half, 0].wait_recv()
            numer_w = numer_w + weigh(chip * 2 + other, half)
        for half in range(HALVES):
            for j in range(1, chips):
                block_copy[half, j].wait_recv()
                came = rounded_ref.at[step, half, chip_at(-j) * 2 + core]
                block_pair[half, j] = send(came, came, block_pair_sem.at[step, half, j], partner)
                numer_w = numer_w + weigh(chip_at(-j) * 2 + core, half)
        gram_h = gram_h_out[step]
        for j in range(1, chips):
            gram_h_copy[j].wait_recv()
            gram_h = gram_h + gram_h_in[step, j]
        gram_h_pair_out[step] = gram_h
        gram_h_pair = send(
            gram_h_pair_out.at[step], gram_h_pair_in.at[step], gram_h_pair_sem.at[step], partner
        )
        for half in range(HALVES):
            for j in range(1, chips):
                block_pair[half, j].wait_recv()
                numer_w = numer_w + weigh(chip_at(-j) * 2 + other, half)
        gram_h_pair.wait_recv()
        gram_h = (gram_h + gram_h_pair_in[step])[:, :rank]
        padded_ref[:, :rank] = numer_w
        basis = (
            basis
            * padded_ref[...].T[:rank, :]
            / (jnp.dot(gram_h, basis, precision=highest, preferred_element_type=jnp.float32) + EPS)
        )
    basis_ref[...] = basis
    for half in range(HALVES):
        profiles_ref[:, half * span : (half + 1) * span] = profiles[half]
    for copy in started:
        copy.wait_send()


def nmf(pixes, feats, spectra, basis, profiles):
    rank, width = profiles.shape
    rows, span = basis.shape[1], width // HALVES
    chips, share = feats // 2, rank // pixes
    f32 = jnp.float32
    dma = pltpu.SemaphoreType.DMA
    return pl.pallas_call(
        functools.partial(nmf_kernel, pixes, chips),
        out_shape=[jax.ShapeDtypeStruct(basis.shape, f32), jax.ShapeDtypeStruct(profiles.shape, f32)],
        in_specs=[pl.BlockSpec(memory_space=pltpu.VMEM)] * 3,
        out_specs=[pl.BlockSpec(memory_space=pltpu.VMEM)] * 2,
        scratch_shapes=[
            pltpu.VMEM((ITERS, HALVES, chips, rank, span), f32),
            pltpu.VMEM((ITERS, HALVES, chips, rank, span), f32),
            pltpu.VMEM((ITERS, rank, LANES), f32),
            pltpu.VMEM((ITERS, rank, LANES), f32),
            pltpu.VMEM((ITERS, HALVES, chips, rank, span + LANES), f32),
            pltpu.VMEM((ITERS, HALVES, chips, rank, span + LANES), f32),
            pltpu.VMEM((ITERS, HALVES, pixes, share, span + LANES), f32),
            pltpu.VMEM((ITERS, HALVES, pixes, share, span + LANES), f32),
            pltpu.VMEM((ITERS, HALVES, pixes, share, span + LANES), f32),
            pltpu.VMEM((ITERS, HALVES, feats, rank, span), jnp.bfloat16),
            pltpu.VMEM((ITERS, rank, LANES), f32),
            pltpu.VMEM((ITERS, chips, rank, LANES), f32),
            pltpu.VMEM((ITERS, rank, LANES), f32),
            pltpu.VMEM((ITERS, rank, LANES), f32),
            pltpu.VMEM((rows, LANES), f32),
            dma((ITERS, HALVES, chips, 2)),
            dma((ITERS, 2)),
            dma((ITERS, HALVES, chips, 2)),
            dma((ITERS, HALVES, pixes, 2)),
            dma((ITERS, HALVES, pixes, 2)),
            dma((ITERS, HALVES, chips, 2)),
            dma((ITERS, HALVES, chips, 2)),
            dma((ITERS, chips, 2)),
            dma((ITERS, 2)),
        ],
        compiler_params=pltpu.CompilerParams(
            collective_id=0, has_side_effects=True, vmem_limit_bytes=44 * 1024 * 1024
        ),
    )(spectra, basis, profiles)


def solution(mesh):
    pixes, feats = mesh.shape["pix"], mesh.shape["feat"]

    def local(mass_bin, mobility_bin, intensity, basis_init, profile_init):
        spectra = bin_peaks(mass_bin, mobility_bin, intensity)
        basis, profiles = nmf(pixes, feats, spectra, basis_init.T, profile_init)
        return (basis.T, profiles)

    return jax.shard_map(
        local,
        mesh=mesh,
        in_specs=(
            P(("pix", "feat"), None),
            P(("pix", "feat"), None),
            P(("pix", "feat"), None),
            P(("pix", "feat"), None),
            P(None, "feat"),
        ),
        out_specs=(P(("pix", "feat"), None), P(None, "feat")),
        check_vma=False,
    )
```

```python
import functools

import jax
import jax.numpy as jnp
from jax import lax
from jax.experimental import pallas as pl
from jax.experimental.pallas import tpu as pltpu
from jax.sharding import PartitionSpec as P

LANES = 128
MZ = 256
MOB = 16
HI = MZ * MOB // LANES
GROUP = 16
CHUNK = 128
ITERS = 2
HALVES = 2
EPS = 1e-06


def bin_peaks(mass_any, mobility_any, weight_any, out_ref, mass_ref, mobility_ref, weight_ref, hi_ref, lo_ref, value_ref, dense_ref, in_sem):
    rows, peaks = mass_any.shape
    hi_iota = lax.broadcasted_iota(jnp.int32, (HI, peaks), 0).astype(jnp.float32).astype(jnp.bfloat16)
    lo_iota = lax.broadcasted_iota(jnp.int32, (LANES, peaks), 0).astype(jnp.float32).astype(jnp.bfloat16)

    def fetches(c):
        own = pl.ds(pl.multiple_of(c * CHUNK, CHUNK), CHUNK)
        pairs = ((mass_any, mass_ref), (mobility_any, mobility_ref), (weight_any, weight_ref))
        return [
            pltpu.make_async_copy(src.at[own], dst.at[own], in_sem.at[c, k])
            for k, (src, dst) in enumerate(pairs)
        ]

    def spread(ref, p, count):
        return jnp.broadcast_to(ref[pl.ds(p, 1), :], (count, peaks)).astype(jnp.bfloat16)

    for c in range(rows // CHUNK):
        for copy in fetches(c):
            copy.start()

    def chunk(c, _):
        for copy in fetches(c):
            copy.wait()
        start = pl.multiple_of(c * CHUNK, CHUNK)
        own = pl.ds(start, CHUNK)
        mass = mass_ref[own, :]
        hi_ref[...] = (mobility_ref[own, :] * (MZ // LANES) + mass // LANES).astype(jnp.float32)
        lo_ref[...] = (mass % LANES).astype(jnp.float32)
        value_ref[...] = weight_ref[own, :].astype(jnp.float32)

        def group(g, _):
            base = pl.multiple_of(g * GROUP, GROUP)
            for i in range(GROUP):
                p = base + i
                left = jnp.where(
                    spread(hi_ref, p, HI) == hi_iota, spread(value_ref, p, HI), jnp.bfloat16(0)
                )
                right = jnp.where(
                    spread(lo_ref, p, LANES) == lo_iota, jnp.bfloat16(1), jnp.bfloat16(0)
                )
                dense_ref[pl.ds(i, HI, stride=GROUP), :] = lax.dot_general(
                    left, right, (((1,), (1,)), ((), ())), preferred_element_type=jnp.float32
                )
            for h in range(HI):
                out_ref[pl.ds(start + base, GROUP), h * LANES : (h + 1) * LANES] = dense_ref[
                    h * GROUP : (h + 1) * GROUP, :
                ].astype(jnp.bfloat16)
            return 0

        lax.fori_loop(0, CHUNK // GROUP, group, 0)
        return 0

    lax.fori_loop(0, rows // CHUNK, chunk, 0)


def nmf_kernel(
    pixes, chips, mass_any, mobility_any, weight_any, basis_in, profiles_in, basis_ref, profiles_ref,
    pair_out, pair_in, gram_out, gram_in, chip_out, chip_in, pix_out, pix_in, whole_ref,
    rounded_ref, gram_h_out, gram_h_in, gram_h_pair_out, gram_h_pair_in, padded_ref,
    pair_sem, gram_sem, chip_sem, pix_sem, whole_sem, block_sem, block_pair_sem, gram_h_sem, gram_h_pair_sem,
    spectra_ref, mass_ref, mobility_ref, weight_ref, hi_ref, lo_ref, value_ref, dense_ref, in_sem,
):
    rank, width = profiles_in.shape
    span = width // HALVES
    share = rank // pixes
    pix, feat = lax.axis_index("pix"), lax.axis_index("feat")
    core, chip = lax.rem(feat, 2), feat // 2
    other = 1 - core
    partner = (pix, chip * 2 + other)
    highest = lax.Precision.HIGHEST

    def chip_at(j):
        return lax.rem(chip + j + chips, chips)

    def pix_at(d):
        return lax.rem(pix + d + pixes, pixes)

    barrier = pltpu.get_barrier_semaphore()
    peers = [partner] + [(pix, chip_at(j) * 2 + core) for j in range(1, chips)]
    peers += [(pix_at(d), feat) for d in range(1, pixes)]
    for peer in peers:
        pl.semaphore_signal(barrier, inc=1, device_id=peer, device_id_type=pl.DeviceIdType.MESH)
    bin_peaks(
        mass_any, mobility_any, weight_any, spectra_ref, mass_ref, mobility_ref, weight_ref,
        hi_ref, lo_ref, value_ref, dense_ref, in_sem,
    )
    pl.semaphore_wait(barrier, len(peers))

    started = []

    def send(src, dst, sems, device):
        copy = pltpu.make_async_remote_copy(
            src_ref=src, dst_ref=dst, send_sem=sems.at[0], recv_sem=sems.at[1],
            device_id=device, device_id_type=pl.DeviceIdType.MESH,
        )
        copy.start()
        started.append(copy)
        return copy

    def columns(block, half):
        return pl.ds(pl.multiple_of(block * width + half * span, LANES), span)

    def reach(half):
        return pl.ds(0, span if half else span + LANES)

    gram_out[...] = jnp.zeros_like(gram_out)
    gram_h_out[...] = jnp.zeros_like(gram_h_out)
    padded_ref[...] = jnp.zeros_like(padded_ref)
    basis = basis_in[...]
    profiles = [profiles_in[:, half * span : (half + 1) * span] for half in range(HALVES)]
    order = list(range(1, chips)) + [0]
    nt = (((1,), (1,)), ((), ()))
    for step in range(ITERS):
        basis_b = basis.astype(jnp.bfloat16)

        def numer(block, half):
            return jnp.dot(
                basis_b, spectra_ref[:, columns(block, half)], preferred_element_type=jnp.float32
            )

        pair, chip_copy, pix_copy, whole_copy, block_copy, block_pair = {}, {}, {}, {}, {}, {}
        for half in range(HALVES):
            for j in order:
                pair_out[step, half, j] = numer(chip_at(j) * 2 + other, half)
                pair[half, j] = send(
                    pair_out.at[step, half, j], pair_in.at[step, half, j], pair_sem.at[step, half, j], partner
                )
            if half == 0:
                gram_out[step, :, :rank] = lax.dot_general(
                    basis, basis, nt, precision=highest, preferred_element_type=jnp.float32
                )
                gram_copy = send(gram_out.at[step], gram_in.at[step], gram_sem.at[step], partner)
            for j in order:
                mine = numer(chip_at(j) * 2 + core, half)
                if half == 0 and j == order[0]:
                    gram_copy.wait_recv()
                    gram = gram_out[step] + gram_in[step]
                pair[half, j].wait_recv()
                chip_out[step, half, j, :, :span] = mine + pair_in[step, half, j]
                if half == 0:
                    chip_out[step, half, j, :, span:] = gram
                if j:
                    chip_copy[half, j] = send(
                        chip_out.at[step, half, j, :, reach(half)],
                        chip_in.at[step, half, j, :, reach(half)],
                        chip_sem.at[step, half, j],
                        (pix, chip_at(j) * 2 + core),
                    )
        for half in range(HALVES):
            size = span if half else span + LANES
            total = chip_out[step, half, 0, :, :size]
            for j in range(1, chips):
                chip_copy[half, j].wait_recv()
                total = total + chip_in[step, half, j, :, :size]
            if share % 8 == 0:
                pix_out[step, half, :, :, :size] = total.reshape(pixes, share, size)
            else:
                for d in range(pixes):
                    pix_out[step, half, d, :, :size] = total[d * share : (d + 1) * share]
            for d in range(1, pixes):
                pix_copy[half, d] = send(
                    pix_out.at[step, half, pix_at(d), :, reach(half)],
                    pix_in.at[step, half, d, :, reach(half)],
                    pix_sem.at[step, half, d],
                    (pix_at(d), feat),
                )
        for half in range(HALVES):
            size = span if half else span + LANES
            part = pix_out[step, half, pix, :, :size]
            for d in range(1, pixes):
                pix_copy[half, d].wait_recv()
                part = part + pix_in[step, half, d, :, :size]
            whole_ref[step, half, pix, :, :size] = part
            for d in range(1, pixes):
                own = whole_ref.at[step, half, pix, :, reach(half)]
                whole_copy[half, d] = send(own, own, whole_sem.at[step, half, d], (pix_at(d), feat))
        for half in range(HALVES):
            size = span if half else span + LANES
            for d in range(1, pixes):
                whole_copy[half, d].wait_recv()
            if share % 8 == 0:
                whole = whole_ref[step, half, :, :, :size].reshape(rank, size)
            else:
                for d in range(pixes):
                    chip_out[step, half, 0, d * share : (d + 1) * share, :size] = whole_ref[step, half, d, :, :size]
                whole = chip_out[step, half, 0, :, :size]
            if half == 0:
                gram_w = whole[:, span : span + rank]
            profiles[half] = (
                profiles[half]
                * whole[:, :span]
                / (jnp.dot(gram_w, profiles[half], precision=highest, preferred_element_type=jnp.float32) + EPS)
            )
            rounded_ref[step, half, feat] = profiles[half].astype(jnp.bfloat16)
            mine = rounded_ref.at[step, half, feat]
            for j in range(1, chips):
                block_copy[half, j] = send(
                    mine, mine, block_sem.at[step, half, j], (pix, chip_at(j) * 2 + core)
                )
            block_pair[half, 0] = send(mine, mine, block_pair_sem.at[step, half, 0], partner)
            part = lax.dot_general(
                profiles[half], profiles[half], nt, precision=highest, preferred_element_type=jnp.float32
            )
            gram_h = gram_h + part if half else part
        gram_h_out[step, :, :rank] = gram_h
        gram_h_copy = {
            j: send(gram_h_out.at[step], gram_h_in.at[step, j], gram_h_sem.at[step, j], (pix, chip_at(j) * 2 + core))
            for j in range(1, chips)
        }

        def weigh(block, half):
            return lax.dot_general(
                spectra_ref[:, columns(block, half)],
                rounded_ref[step, half, block],
                nt,
                preferred_element_type=jnp.float32,
            )

        numer_w = weigh(feat, 0)
        for half in range(1, HALVES):
            numer_w = numer_w + weigh(feat, half)
        for half in range(HALVES):
            block_pair[half, 0].wait_recv()
            numer_w = numer_w + weigh(chip * 2 + other, half)
        for half in range(HALVES):
            for j in range(1, chips):
                block_copy[half, j].wait_recv()
                came = rounded_ref.at[step, half, chip_at(-j) * 2 + core]
                block_pair[half, j] = send(came, came, block_pair_sem.at[step, half, j], partner)
                numer_w = numer_w + weigh(chip_at(-j) * 2 + core, half)
        gram_h = gram_h_out[step]
        for j in range(1, chips):
            gram_h_copy[j].wait_recv()
            gram_h = gram_h + gram_h_in[step, j]
        gram_h_pair_out[step] = gram_h
        gram_h_pair = send(
            gram_h_pair_out.at[step], gram_h_pair_in.at[step], gram_h_pair_sem.at[step], partner
        )
        for half in range(HALVES):
            for j in range(1, chips):
                block_pair[half, j].wait_recv()
                numer_w = numer_w + weigh(chip_at(-j) * 2 + other, half)
        gram_h_pair.wait_recv()
        gram_h = (gram_h + gram_h_pair_in[step])[:, :rank]
        padded_ref[:, :rank] = numer_w
        basis = (
            basis
            * padded_ref[...].T[:rank, :]
            / (jnp.dot(gram_h, basis, precision=highest, preferred_element_type=jnp.float32) + EPS)
        )
    basis_ref[...] = basis
    for half in range(HALVES):
        profiles_ref[:, half * span : (half + 1) * span] = profiles[half]
    for copy in started:
        copy.wait_send()


def nmf(pixes, feats, mass, mobility, weight, basis, profiles):
    rank, width = profiles.shape
    rows, span = basis.shape[1], width // HALVES
    chips, share = feats // 2, rank // pixes
    f32 = jnp.float32
    peaks = mass.shape[1]
    dma = pltpu.SemaphoreType.DMA
    return pl.pallas_call(
        functools.partial(nmf_kernel, pixes, chips),
        out_shape=[jax.ShapeDtypeStruct(basis.shape, f32), jax.ShapeDtypeStruct(profiles.shape, f32)],
        in_specs=[pl.BlockSpec(memory_space=pl.ANY)] * 3 + [pl.BlockSpec(memory_space=pltpu.VMEM)] * 2,
        out_specs=[pl.BlockSpec(memory_space=pltpu.VMEM)] * 2,
        scratch_shapes=[
            pltpu.VMEM((ITERS, HALVES, chips, rank, span), f32),
            pltpu.VMEM((ITERS, HALVES, chips, rank, span), f32),
            pltpu.VMEM((ITERS, rank, LANES), f32),
            pltpu.VMEM((ITERS, rank, LANES), f32),
            pltpu.VMEM((ITERS, HALVES, chips, rank, span + LANES), f32),
            pltpu.VMEM((ITERS, HALVES, chips, rank, span + LANES), f32),
            pltpu.VMEM((ITERS, HALVES, pixes, share, span + LANES), f32),
            pltpu.VMEM((ITERS, HALVES, pixes, share, span + LANES), f32),
            pltpu.VMEM((ITERS, HALVES, pixes, share, span + LANES), f32),
            pltpu.VMEM((ITERS, HALVES, feats, rank, span), jnp.bfloat16),
            pltpu.VMEM((ITERS, rank, LANES), f32),
            pltpu.VMEM((ITERS, chips, rank, LANES), f32),
            pltpu.VMEM((ITERS, rank, LANES), f32),
            pltpu.VMEM((ITERS, rank, LANES), f32),
            pltpu.VMEM((rows, LANES), f32),
            dma((ITERS, HALVES, chips, 2)),
            dma((ITERS, 2)),
            dma((ITERS, HALVES, chips, 2)),
            dma((ITERS, HALVES, pixes, 2)),
            dma((ITERS, HALVES, pixes, 2)),
            dma((ITERS, HALVES, chips, 2)),
            dma((ITERS, HALVES, chips, 2)),
            dma((ITERS, chips, 2)),
            dma((ITERS, 2)),
            pltpu.VMEM((rows, MZ * MOB), jnp.bfloat16),
            pltpu.VMEM((rows, peaks), jnp.int32),
            pltpu.VMEM((rows, peaks), jnp.int32),
            pltpu.VMEM((rows, peaks), jnp.bfloat16),
            pltpu.VMEM((CHUNK, peaks), f32),
            pltpu.VMEM((CHUNK, peaks), f32),
            pltpu.VMEM((CHUNK, peaks), f32),
            pltpu.VMEM((HI * GROUP, LANES), f32),
            dma((rows // CHUNK, 3)),
        ],
        compiler_params=pltpu.CompilerParams(
            collective_id=0, has_side_effects=True, vmem_limit_bytes=44 * 1024 * 1024
        ),
    )(mass, mobility, weight, basis, profiles)


def solution(mesh):
    pixes, feats = mesh.shape["pix"], mesh.shape["feat"]

    def local(mass_bin, mobility_bin, intensity, basis_init, profile_init):
        basis, profiles = nmf(
            pixes, feats, mass_bin, mobility_bin, intensity, basis_init.T, profile_init
        )
        return (basis.T, profiles)

    return jax.shard_map(
        local,
        mesh=mesh,
        in_specs=(
            P(("pix", "feat"), None),
            P(("pix", "feat"), None),
            P(("pix", "feat"), None),
            P(("pix", "feat"), None),
            P(None, "feat"),
        ),
        out_specs=(P(("pix", "feat"), None), P(None, "feat")),
        check_vma=False,
    )
```

```python
import functools

import jax
import jax.numpy as jnp
from jax import lax
from jax.experimental import pallas as pl
from jax.experimental.pallas import tpu as pltpu
from jax.sharding import PartitionSpec as P

LANES = 128
MZ = 256
MOB = 16
HI = MZ * MOB // LANES
GROUP = 16
CHUNK = 128
ITERS = 2
HALVES = 2
EPS = 1e-06


def bin_peaks(mass_any, mobility_any, weight_any, out_ref, mass_ref, mobility_ref, weight_ref, hi_ref, lo_ref, value_ref, dense_ref, in_sem):
    rows, peaks = mass_any.shape
    hi_iota = lax.broadcasted_iota(jnp.int32, (HI, peaks), 0).astype(jnp.float32).astype(jnp.bfloat16)
    lo_iota = lax.broadcasted_iota(jnp.int32, (LANES, peaks), 0).astype(jnp.float32).astype(jnp.bfloat16)

    def fetches(c):
        own = pl.ds(pl.multiple_of(c * CHUNK, CHUNK), CHUNK)
        pairs = ((mass_any, mass_ref), (mobility_any, mobility_ref), (weight_any, weight_ref))
        return [
            pltpu.make_async_copy(src.at[own], dst.at[own], in_sem.at[c, k])
            for k, (src, dst) in enumerate(pairs)
        ]

    def spread(ref, p, count):
        return jnp.broadcast_to(ref[pl.ds(p, 1), :], (count, peaks)).astype(jnp.bfloat16)

    for c in range(rows // CHUNK):
        for copy in fetches(c):
            copy.start()

    def chunk(c, _):
        for copy in fetches(c):
            copy.wait()
        start = pl.multiple_of(c * CHUNK, CHUNK)
        own = pl.ds(start, CHUNK)
        mass = mass_ref[own, :]
        hi_ref[...] = (mobility_ref[own, :] * (MZ // LANES) + mass // LANES).astype(jnp.float32)
        lo_ref[...] = (mass % LANES).astype(jnp.float32)
        value_ref[...] = weight_ref[own, :].astype(jnp.float32)

        def group(g, _):
            base = pl.multiple_of(g * GROUP, GROUP)
            for i in range(0, GROUP, 2):
                left, right = [], []
                for p in (base + i, base + i + 1):
                    left.append(
                        jnp.where(
                            spread(hi_ref, p, HI) == hi_iota, spread(value_ref, p, HI), jnp.bfloat16(0)
                        )
                    )
                    right.append(
                        jnp.where(
                            spread(lo_ref, p, LANES) == lo_iota, jnp.bfloat16(1), jnp.bfloat16(0)
                        )
                    )
                both = lax.dot_general(
                    jnp.concatenate(left, 0),
                    jnp.concatenate(right, 0),
                    (((1,), (1,)), ((), ())),
                    preferred_element_type=jnp.float32,
                )
                dense_ref[pl.ds(i, HI, stride=GROUP), :] = both[:HI, :LANES]
                dense_ref[pl.ds(i + 1, HI, stride=GROUP), :] = both[HI:, LANES:]
            for h in range(HI):
                out_ref[pl.ds(start + base, GROUP), h * LANES : (h + 1) * LANES] = dense_ref[
                    h * GROUP : (h + 1) * GROUP, :
                ].astype(jnp.bfloat16)
            return 0

        lax.fori_loop(0, CHUNK // GROUP, group, 0)
        return 0

    lax.fori_loop(0, rows // CHUNK, chunk, 0)


def nmf_kernel(
    pixes, chips, mass_any, mobility_any, weight_any, basis_any, profiles_any, basis_ref, profiles_ref,
    pair_out, pair_in, gram_out, gram_in, chip_out, chip_in, pix_out, pix_in, whole_ref,
    rounded_ref, gram_h_out, gram_h_in, gram_h_pair_out, gram_h_pair_in, padded_ref,
    pair_sem, gram_sem, chip_sem, pix_sem, whole_sem, block_sem, block_pair_sem, gram_h_sem, gram_h_pair_sem,
    spectra_ref, mass_ref, mobility_ref, weight_ref, hi_ref, lo_ref, value_ref, dense_ref, in_sem,
    basis_in, profiles_in, start_sem,
):
    rank, width = profiles_any.shape
    span = width // HALVES
    share = rank // pixes
    pix, feat = lax.axis_index("pix"), lax.axis_index("feat")
    core, chip = lax.rem(feat, 2), feat // 2
    other = 1 - core
    partner = (pix, chip * 2 + other)
    highest = lax.Precision.HIGHEST

    def chip_at(j):
        return lax.rem(chip + j + chips, chips)

    def pix_at(d):
        return lax.rem(pix + d + pixes, pixes)

    barrier = pltpu.get_barrier_semaphore()
    peers = [partner] + [(pix, chip_at(j) * 2 + core) for j in range(1, chips)]
    peers += [(pix_at(d), feat) for d in range(1, pixes)]
    for peer in peers:
        pl.semaphore_signal(barrier, inc=1, device_id=peer, device_id_type=pl.DeviceIdType.MESH)
    starts = [
        pltpu.make_async_copy(basis_any, basis_in, start_sem.at[0]),
        pltpu.make_async_copy(profiles_any, profiles_in, start_sem.at[1]),
    ]
    for copy in starts:
        copy.start()
    bin_peaks(
        mass_any, mobility_any, weight_any, spectra_ref, mass_ref, mobility_ref, weight_ref,
        hi_ref, lo_ref, value_ref, dense_ref, in_sem,
    )
    for copy in starts:
        copy.wait()
    pl.semaphore_wait(barrier, len(peers))

    started = []

    def send(src, dst, sems, device):
        copy = pltpu.make_async_remote_copy(
            src_ref=src, dst_ref=dst, send_sem=sems.at[0], recv_sem=sems.at[1],
            device_id=device, device_id_type=pl.DeviceIdType.MESH,
        )
        copy.start()
        started.append(copy)
        return copy

    def columns(block, half):
        return pl.ds(pl.multiple_of(block * width + half * span, LANES), span)

    def reach(half):
        return pl.ds(0, span if half else span + LANES)

    gram_out[...] = jnp.zeros_like(gram_out)
    gram_h_out[...] = jnp.zeros_like(gram_h_out)
    padded_ref[...] = jnp.zeros_like(padded_ref)
    basis = basis_in[...]
    profiles = [profiles_in[:, half * span : (half + 1) * span] for half in range(HALVES)]
    order = list(range(1, chips)) + [0]
    nt = (((1,), (1,)), ((), ()))
    for step in range(ITERS):
        basis_b = basis.astype(jnp.bfloat16)

        def numer(block, half):
            return jnp.dot(
                basis_b, spectra_ref[:, columns(block, half)], preferred_element_type=jnp.float32
            )

        pair, chip_copy, pix_copy, whole_copy, block_copy, block_pair = {}, {}, {}, {}, {}, {}
        for half in range(HALVES):
            for j in order:
                pair_out[step, half, j] = numer(chip_at(j) * 2 + other, half)
                pair[half, j] = send(
                    pair_out.at[step, half, j], pair_in.at[step, half, j], pair_sem.at[step, half, j], partner
                )
            if half == 0:
                gram_out[step, :, :rank] = lax.dot_general(
                    basis, basis, nt, precision=highest, preferred_element_type=jnp.float32
                )
                gram_copy = send(gram_out.at[step], gram_in.at[step], gram_sem.at[step], partner)
            for j in order:
                mine = numer(chip_at(j) * 2 + core, half)
                if half == 0 and j == order[0]:
                    gram_copy.wait_recv()
                    gram = gram_out[step] + gram_in[step]
                pair[half, j].wait_recv()
                chip_out[step, half, j, :, :span] = mine + pair_in[step, half, j]
                if half == 0:
                    chip_out[step, half, j, :, span:] = gram
                if j:
                    chip_copy[half, j] = send(
                        chip_out.at[step, half, j, :, reach(half)],
                        chip_in.at[step, half, j, :, reach(half)],
                        chip_sem.at[step, half, j],
                        (pix, chip_at(j) * 2 + core),
                    )
        for half in range(HALVES):
            size = span if half else span + LANES
            total = chip_out[step, half, 0, :, :size]
            for j in range(1, chips):
                chip_copy[half, j].wait_recv()
                total = total + chip_in[step, half, j, :, :size]
            if share % 8 == 0:
                pix_out[step, half, :, :, :size] = total.reshape(pixes, share, size)
            else:
                for d in range(pixes):
                    pix_out[step, half, d, :, :size] = total[d * share : (d + 1) * share]
            for d in range(1, pixes):
                pix_copy[half, d] = send(
                    pix_out.at[step, half, pix_at(d), :, reach(half)],
                    pix_in.at[step, half, d, :, reach(half)],
                    pix_sem.at[step, half, d],
                    (pix_at(d), feat),
                )
        for half in range(HALVES):
            size = span if half else span + LANES
            part = pix_out[step, half, pix, :, :size]
            for d in range(1, pixes):
                pix_copy[half, d].wait_recv()
                part = part + pix_in[step, half, d, :, :size]
            whole_ref[step, half, pix, :, :size] = part
            for d in range(1, pixes):
                own = whole_ref.at[step, half, pix, :, reach(half)]
                whole_copy[half, d] = send(own, own, whole_sem.at[step, half, d], (pix_at(d), feat))
        for half in range(HALVES):
            size = span if half else span + LANES
            for d in range(1, pixes):
                whole_copy[half, d].wait_recv()
            if share % 8 == 0:
                whole = whole_ref[step, half, :, :, :size].reshape(rank, size)
            else:
                for d in range(pixes):
                    chip_out[step, half, 0, d * share : (d + 1) * share, :size] = whole_ref[step, half, d, :, :size]
                whole = chip_out[step, half, 0, :, :size]
            if half == 0:
                gram_w = whole[:, span : span + rank]
            profiles[half] = (
                profiles[half]
                * whole[:, :span]
                / (jnp.dot(gram_w, profiles[half], precision=highest, preferred_element_type=jnp.float32) + EPS)
            )
            rounded_ref[step, half, feat] = profiles[half].astype(jnp.bfloat16)
            mine = rounded_ref.at[step, half, feat]
            for j in range(1, chips):
                block_copy[half, j] = send(
                    mine, mine, block_sem.at[step, half, j], (pix, chip_at(j) * 2 + core)
                )
            block_pair[half, 0] = send(mine, mine, block_pair_sem.at[step, half, 0], partner)
            part = lax.dot_general(
                profiles[half], profiles[half], nt, precision=highest, preferred_element_type=jnp.float32
            )
            gram_h = gram_h + part if half else part
        gram_h_out[step, :, :rank] = gram_h
        gram_h_copy = {
            j: send(gram_h_out.at[step], gram_h_in.at[step, j], gram_h_sem.at[step, j], (pix, chip_at(j) * 2 + core))
            for j in range(1, chips)
        }

        def weigh(block, half):
            return lax.dot_general(
                spectra_ref[:, columns(block, half)],
                rounded_ref[step, half, block],
                nt,
                preferred_element_type=jnp.float32,
            )

        numer_w = weigh(feat, 0)
        for half in range(1, HALVES):
            numer_w = numer_w + weigh(feat, half)
        for half in range(HALVES):
            block_pair[half, 0].wait_recv()
            numer_w = numer_w + weigh(chip * 2 + other, half)
        for half in range(HALVES):
            for j in range(1, chips):
                block_copy[half, j].wait_recv()
                came = rounded_ref.at[step, half, chip_at(-j) * 2 + core]
                block_pair[half, j] = send(came, came, block_pair_sem.at[step, half, j], partner)
                numer_w = numer_w + weigh(chip_at(-j) * 2 + core, half)
        gram_h = gram_h_out[step]
        for j in range(1, chips):
            gram_h_copy[j].wait_recv()
            gram_h = gram_h + gram_h_in[step, j]
        gram_h_pair_out[step] = gram_h
        gram_h_pair = send(
            gram_h_pair_out.at[step], gram_h_pair_in.at[step], gram_h_pair_sem.at[step], partner
        )
        for half in range(HALVES):
            for j in range(1, chips):
                block_pair[half, j].wait_recv()
                numer_w = numer_w + weigh(chip_at(-j) * 2 + other, half)
        gram_h_pair.wait_recv()
        gram_h = (gram_h + gram_h_pair_in[step])[:, :rank]
        padded_ref[:, :rank] = numer_w
        basis = (
            basis
            * padded_ref[...].T[:rank, :]
            / (jnp.dot(gram_h, basis, precision=highest, preferred_element_type=jnp.float32) + EPS)
        )
    basis_ref[...] = basis
    for half in range(HALVES):
        profiles_ref[:, half * span : (half + 1) * span] = profiles[half]
    for copy in started:
        copy.wait_send()


def nmf(pixes, feats, mass, mobility, weight, basis, profiles):
    rank, width = profiles.shape
    rows, span = basis.shape[1], width // HALVES
    chips, share = feats // 2, rank // pixes
    f32 = jnp.float32
    peaks = mass.shape[1]
    dma = pltpu.SemaphoreType.DMA
    return pl.pallas_call(
        functools.partial(nmf_kernel, pixes, chips),
        out_shape=[jax.ShapeDtypeStruct(basis.shape, f32), jax.ShapeDtypeStruct(profiles.shape, f32)],
        in_specs=[pl.BlockSpec(memory_space=pltpu.HBM)] * 5,
        out_specs=[pl.BlockSpec(memory_space=pltpu.VMEM)] * 2,
        scratch_shapes=[
            pltpu.VMEM((ITERS, HALVES, chips, rank, span), f32),
            pltpu.VMEM((ITERS, HALVES, chips, rank, span), f32),
            pltpu.VMEM((ITERS, rank, LANES), f32),
            pltpu.VMEM((ITERS, rank, LANES), f32),
            pltpu.VMEM((ITERS, HALVES, chips, rank, span + LANES), f32),
            pltpu.VMEM((ITERS, HALVES, chips, rank, span + LANES), f32),
            pltpu.VMEM((ITERS, HALVES, pixes, share, span + LANES), f32),
            pltpu.VMEM((ITERS, HALVES, pixes, share, span + LANES), f32),
            pltpu.VMEM((ITERS, HALVES, pixes, share, span + LANES), f32),
            pltpu.VMEM((ITERS, HALVES, feats, rank, span), jnp.bfloat16),
            pltpu.VMEM((ITERS, rank, LANES), f32),
            pltpu.VMEM((ITERS, chips, rank, LANES), f32),
            pltpu.VMEM((ITERS, rank, LANES), f32),
            pltpu.VMEM((ITERS, rank, LANES), f32),
            pltpu.VMEM((rows, LANES), f32),
            dma((ITERS, HALVES, chips, 2)),
            dma((ITERS, 2)),
            dma((ITERS, HALVES, chips, 2)),
            dma((ITERS, HALVES, pixes, 2)),
            dma((ITERS, HALVES, pixes, 2)),
            dma((ITERS, HALVES, chips, 2)),
            dma((ITERS, HALVES, chips, 2)),
            dma((ITERS, chips, 2)),
            dma((ITERS, 2)),
            pltpu.VMEM((rows, MZ * MOB), jnp.bfloat16),
            pltpu.VMEM((rows, peaks), jnp.int32),
            pltpu.VMEM((rows, peaks), jnp.int32),
            pltpu.VMEM((rows, peaks), jnp.bfloat16),
            pltpu.VMEM((CHUNK, peaks), f32),
            pltpu.VMEM((CHUNK, peaks), f32),
            pltpu.VMEM((CHUNK, peaks), f32),
            pltpu.VMEM((HI * GROUP, LANES), f32),
            dma((rows // CHUNK, 3)),
            pltpu.VMEM((rank, rows), f32),
            pltpu.VMEM((rank, width), f32),
            dma((2,)),
        ],
        compiler_params=pltpu.CompilerParams(
            collective_id=0, has_side_effects=True, vmem_limit_bytes=44 * 1024 * 1024
        ),
    )(mass, mobility, weight, basis, profiles)


def solution(mesh):
    pixes, feats = mesh.shape["pix"], mesh.shape["feat"]

    def local(mass_bin, mobility_bin, intensity, basis_init, profile_init):
        basis, profiles = nmf(
            pixes, feats, mass_bin, mobility_bin, intensity, basis_init.T, profile_init
        )
        return (basis.T, profiles)

    return jax.shard_map(
        local,
        mesh=mesh,
        in_specs=(
            P(("pix", "feat"), None),
            P(("pix", "feat"), None),
            P(("pix", "feat"), None),
            P(("pix", "feat"), None),
            P(None, "feat"),
        ),
        out_specs=(P(("pix", "feat"), None), P(None, "feat")),
        check_vma=False,
    )
```

```python
import functools

import jax
import jax.numpy as jnp
from jax import lax
from jax.experimental import pallas as pl
from jax.experimental.pallas import tpu as pltpu
from jax.sharding import PartitionSpec as P

LANES = 128
MZ = 256
MOB = 16
HI = MZ * MOB // LANES
GROUP = 16
CHUNK = 128
ITERS = 2
HALVES = 2
EPS = 1e-06


def bin_peaks(mass_any, mobility_any, weight_any, out_ref, mass_ref, mobility_ref, weight_ref, hi_ref, lo_ref, value_ref, dense_ref, in_sem):
    rows, peaks = mass_any.shape
    hi_iota = lax.broadcasted_iota(jnp.int32, (HI, peaks), 0).astype(jnp.float32).astype(jnp.bfloat16)
    lo_iota = lax.broadcasted_iota(jnp.int32, (LANES, peaks), 0).astype(jnp.float32).astype(jnp.bfloat16)

    def fetches(c):
        own = pl.ds(pl.multiple_of(c * CHUNK, CHUNK), CHUNK)
        pairs = ((mass_any, mass_ref), (mobility_any, mobility_ref), (weight_any, weight_ref))
        return [
            pltpu.make_async_copy(src.at[own], dst.at[own], in_sem.at[c, k])
            for k, (src, dst) in enumerate(pairs)
        ]

    def spread(ref, p, count):
        return jnp.broadcast_to(ref[pl.ds(p, 1), :], (count, peaks)).astype(jnp.bfloat16)

    for c in range(rows // CHUNK):
        for copy in fetches(c):
            copy.start()

    def chunk(c, _):
        for copy in fetches(c):
            copy.wait()
        start = pl.multiple_of(c * CHUNK, CHUNK)
        own = pl.ds(start, CHUNK)
        mass = mass_ref[own, :]
        hi_ref[...] = (mobility_ref[own, :] * (MZ // LANES) + mass // LANES).astype(jnp.float32)
        lo_ref[...] = (mass % LANES).astype(jnp.float32)
        value_ref[...] = weight_ref[own, :].astype(jnp.float32)

        def group(g, _):
            base = pl.multiple_of(g * GROUP, GROUP)
            for i in range(0, GROUP, 2):
                left, right = [], []
                for p in (base + i, base + i + 1):
                    left.append(
                        jnp.where(
                            spread(hi_ref, p, HI) == hi_iota, spread(value_ref, p, HI), jnp.bfloat16(0)
                        )
                    )
                    away = spread(lo_ref, p, LANES) - lo_iota
                    right.append(jnp.maximum(jnp.bfloat16(1) - away * away, jnp.bfloat16(0)))
                both = lax.dot_general(
                    jnp.concatenate(left, 0),
                    jnp.concatenate(right, 0),
                    (((1,), (1,)), ((), ())),
                    preferred_element_type=jnp.float32,
                )
                dense_ref[pl.ds(i, HI, stride=GROUP), :] = both[:HI, :LANES]
                dense_ref[pl.ds(i + 1, HI, stride=GROUP), :] = both[HI:, LANES:]
            for h in range(HI):
                out_ref[pl.ds(start + base, GROUP), h * LANES : (h + 1) * LANES] = dense_ref[
                    h * GROUP : (h + 1) * GROUP, :
                ].astype(jnp.bfloat16)
            return 0

        lax.fori_loop(0, CHUNK // GROUP, group, 0)
        return 0

    lax.fori_loop(0, rows // CHUNK, chunk, 0)


def nmf_kernel(
    pixes, chips, mass_any, mobility_any, weight_any, basis_any, profiles_any, basis_ref, profiles_ref,
    pair_out, pair_in, gram_out, gram_in, chip_out, chip_in, pix_out, pix_in, whole_ref,
    rounded_ref, gram_h_out, gram_h_in, gram_h_pair_out, gram_h_pair_in, padded_ref,
    pair_sem, gram_sem, chip_sem, pix_sem, whole_sem, block_sem, block_pair_sem, gram_h_sem, gram_h_pair_sem,
    spectra_ref, mass_ref, mobility_ref, weight_ref, hi_ref, lo_ref, value_ref, dense_ref, in_sem,
    basis_in, profiles_in, start_sem,
):
    rank, width = profiles_any.shape
    span = width // HALVES
    share = rank // pixes
    pix, feat = lax.axis_index("pix"), lax.axis_index("feat")
    core, chip = lax.rem(feat, 2), feat // 2
    other = 1 - core
    partner = (pix, chip * 2 + other)
    highest = lax.Precision.HIGHEST

    def chip_at(j):
        return lax.rem(chip + j + chips, chips)

    def pix_at(d):
        return lax.rem(pix + d + pixes, pixes)

    barrier = pltpu.get_barrier_semaphore()
    peers = [partner] + [(pix, chip_at(j) * 2 + core) for j in range(1, chips)]
    peers += [(pix_at(d), feat) for d in range(1, pixes)]
    for peer in peers:
        pl.semaphore_signal(barrier, inc=1, device_id=peer, device_id_type=pl.DeviceIdType.MESH)
    starts = [
        pltpu.make_async_copy(basis_any, basis_in, start_sem.at[0]),
        pltpu.make_async_copy(profiles_any, profiles_in, start_sem.at[1]),
    ]
    for copy in starts:
        copy.start()
    bin_peaks(
        mass_any, mobility_any, weight_any, spectra_ref, mass_ref, mobility_ref, weight_ref,
        hi_ref, lo_ref, value_ref, dense_ref, in_sem,
    )
    for copy in starts:
        copy.wait()
    pl.semaphore_wait(barrier, len(peers))

    started = []

    def send(src, dst, sems, device):
        copy = pltpu.make_async_remote_copy(
            src_ref=src, dst_ref=dst, send_sem=sems.at[0], recv_sem=sems.at[1],
            device_id=device, device_id_type=pl.DeviceIdType.MESH,
        )
        copy.start()
        started.append(copy)
        return copy

    def columns(block, half):
        return pl.ds(pl.multiple_of(block * width + half * span, LANES), span)

    def reach(half):
        return pl.ds(0, span if half else span + LANES)

    gram_out[...] = jnp.zeros_like(gram_out)
    gram_h_out[...] = jnp.zeros_like(gram_h_out)
    padded_ref[...] = jnp.zeros_like(padded_ref)
    basis = basis_in[...]
    profiles = [profiles_in[:, half * span : (half + 1) * span] for half in range(HALVES)]
    order = list(range(1, chips)) + [0]
    nt = (((1,), (1,)), ((), ()))
    for step in range(ITERS):
        basis_b = basis.astype(jnp.bfloat16)

        def numer(block, half):
            return jnp.dot(
                basis_b, spectra_ref[:, columns(block, half)], preferred_element_type=jnp.float32
            )

        pair, chip_copy, pix_copy, whole_copy, block_copy, block_pair = {}, {}, {}, {}, {}, {}
        for half in range(HALVES):
            for j in order:
                pair_out[step, half, j] = numer(chip_at(j) * 2 + other, half)
                pair[half, j] = send(
                    pair_out.at[step, half, j], pair_in.at[step, half, j], pair_sem.at[step, half, j], partner
                )
            if half == 0:
                gram_out[step, :, :rank] = lax.dot_general(
                    basis, basis, nt, precision=highest, preferred_element_type=jnp.float32
                )
                gram_copy = send(gram_out.at[step], gram_in.at[step], gram_sem.at[step], partner)
            for j in order:
                mine = numer(chip_at(j) * 2 + core, half)
                if half == 0 and j == order[0]:
                    gram_copy.wait_recv()
                    gram = gram_out[step] + gram_in[step]
                pair[half, j].wait_recv()
                chip_out[step, half, j, :, :span] = mine + pair_in[step, half, j]
                if half == 0:
                    chip_out[step, half, j, :, span:] = gram
                if j:
                    chip_copy[half, j] = send(
                        chip_out.at[step, half, j, :, reach(half)],
                        chip_in.at[step, half, j, :, reach(half)],
                        chip_sem.at[step, half, j],
                        (pix, chip_at(j) * 2 + core),
                    )
        for half in range(HALVES):
            size = span if half else span + LANES
            total = chip_out[step, half, 0, :, :size]
            for j in range(1, chips):
                chip_copy[half, j].wait_recv()
                total = total + chip_in[step, half, j, :, :size]
            if share % 8 == 0:
                pix_out[step, half, :, :, :size] = total.reshape(pixes, share, size)
            else:
                for d in range(pixes):
                    pix_out[step, half, d, :, :size] = total[d * share : (d + 1) * share]
            for d in range(1, pixes):
                pix_copy[half, d] = send(
                    pix_out.at[step, half, pix_at(d), :, reach(half)],
                    pix_in.at[step, half, d, :, reach(half)],
                    pix_sem.at[step, half, d],
                    (pix_at(d), feat),
                )
        for half in range(HALVES):
            size = span if half else span + LANES
            part = pix_out[step, half, pix, :, :size]
            for d in range(1, pixes):
                pix_copy[half, d].wait_recv()
                part = part + pix_in[step, half, d, :, :size]
            whole_ref[step, half, pix, :, :size] = part
            for d in range(1, pixes):
                own = whole_ref.at[step, half, pix, :, reach(half)]
                whole_copy[half, d] = send(own, own, whole_sem.at[step, half, d], (pix_at(d), feat))
        for half in range(HALVES):
            size = span if half else span + LANES
            for d in range(1, pixes):
                whole_copy[half, d].wait_recv()
            if share % 8 == 0:
                whole = whole_ref[step, half, :, :, :size].reshape(rank, size)
            else:
                for d in range(pixes):
                    chip_out[step, half, 0, d * share : (d + 1) * share, :size] = whole_ref[step, half, d, :, :size]
                whole = chip_out[step, half, 0, :, :size]
            if half == 0:
                gram_w = whole[:, span : span + rank]
            profiles[half] = (
                profiles[half]
                * whole[:, :span]
                / (jnp.dot(gram_w, profiles[half], precision=highest, preferred_element_type=jnp.float32) + EPS)
            )
            rounded_ref[step, half, feat] = profiles[half].astype(jnp.bfloat16)
            mine = rounded_ref.at[step, half, feat]
            for j in range(1, chips):
                block_copy[half, j] = send(
                    mine, mine, block_sem.at[step, half, j], (pix, chip_at(j) * 2 + core)
                )
            block_pair[half, 0] = send(mine, mine, block_pair_sem.at[step, half, 0], partner)
            part = lax.dot_general(
                profiles[half], profiles[half], nt, precision=highest, preferred_element_type=jnp.float32
            )
            gram_h = gram_h + part if half else part
        gram_h_out[step, :, :rank] = gram_h
        gram_h_copy = {
            j: send(gram_h_out.at[step], gram_h_in.at[step, j], gram_h_sem.at[step, j], (pix, chip_at(j) * 2 + core))
            for j in range(1, chips)
        }

        def weigh(block, half):
            return lax.dot_general(
                spectra_ref[:, columns(block, half)],
                rounded_ref[step, half, block],
                nt,
                preferred_element_type=jnp.float32,
            )

        numer_w = weigh(feat, 0)
        for half in range(1, HALVES):
            numer_w = numer_w + weigh(feat, half)
        for half in range(HALVES):
            block_pair[half, 0].wait_recv()
            numer_w = numer_w + weigh(chip * 2 + other, half)
        for half in range(HALVES):
            for j in range(1, chips):
                block_copy[half, j].wait_recv()
                came = rounded_ref.at[step, half, chip_at(-j) * 2 + core]
                block_pair[half, j] = send(came, came, block_pair_sem.at[step, half, j], partner)
                numer_w = numer_w + weigh(chip_at(-j) * 2 + core, half)
        gram_h = gram_h_out[step]
        for j in range(1, chips):
            gram_h_copy[j].wait_recv()
            gram_h = gram_h + gram_h_in[step, j]
        gram_h_pair_out[step] = gram_h
        gram_h_pair = send(
            gram_h_pair_out.at[step], gram_h_pair_in.at[step], gram_h_pair_sem.at[step], partner
        )
        for half in range(HALVES):
            for j in range(1, chips):
                block_pair[half, j].wait_recv()
                numer_w = numer_w + weigh(chip_at(-j) * 2 + other, half)
        gram_h_pair.wait_recv()
        gram_h = (gram_h + gram_h_pair_in[step])[:, :rank]
        padded_ref[:, :rank] = numer_w
        basis = (
            basis
            * padded_ref[...].T[:rank, :]
            / (jnp.dot(gram_h, basis, precision=highest, preferred_element_type=jnp.float32) + EPS)
        )
    basis_ref[...] = basis
    for half in range(HALVES):
        profiles_ref[:, half * span : (half + 1) * span] = profiles[half]
    for copy in started:
        copy.wait_send()


def nmf(pixes, feats, mass, mobility, weight, basis, profiles):
    rank, width = profiles.shape
    rows, span = basis.shape[1], width // HALVES
    chips, share = feats // 2, rank // pixes
    f32 = jnp.float32
    peaks = mass.shape[1]
    dma = pltpu.SemaphoreType.DMA
    return pl.pallas_call(
        functools.partial(nmf_kernel, pixes, chips),
        out_shape=[jax.ShapeDtypeStruct(basis.shape, f32), jax.ShapeDtypeStruct(profiles.shape, f32)],
        in_specs=[pl.BlockSpec(memory_space=pltpu.HBM)] * 5,
        out_specs=[pl.BlockSpec(memory_space=pltpu.VMEM)] * 2,
        scratch_shapes=[
            pltpu.VMEM((ITERS, HALVES, chips, rank, span), f32),
            pltpu.VMEM((ITERS, HALVES, chips, rank, span), f32),
            pltpu.VMEM((ITERS, rank, LANES), f32),
            pltpu.VMEM((ITERS, rank, LANES), f32),
            pltpu.VMEM((ITERS, HALVES, chips, rank, span + LANES), f32),
            pltpu.VMEM((ITERS, HALVES, chips, rank, span + LANES), f32),
            pltpu.VMEM((ITERS, HALVES, pixes, share, span + LANES), f32),
            pltpu.VMEM((ITERS, HALVES, pixes, share, span + LANES), f32),
            pltpu.VMEM((ITERS, HALVES, pixes, share, span + LANES), f32),
            pltpu.VMEM((ITERS, HALVES, feats, rank, span), jnp.bfloat16),
            pltpu.VMEM((ITERS, rank, LANES), f32),
            pltpu.VMEM((ITERS, chips, rank, LANES), f32),
            pltpu.VMEM((ITERS, rank, LANES), f32),
            pltpu.VMEM((ITERS, rank, LANES), f32),
            pltpu.VMEM((rows, LANES), f32),
            dma((ITERS, HALVES, chips, 2)),
            dma((ITERS, 2)),
            dma((ITERS, HALVES, chips, 2)),
            dma((ITERS, HALVES, pixes, 2)),
            dma((ITERS, HALVES, pixes, 2)),
            dma((ITERS, HALVES, chips, 2)),
            dma((ITERS, HALVES, chips, 2)),
            dma((ITERS, chips, 2)),
            dma((ITERS, 2)),
            pltpu.VMEM((rows, MZ * MOB), jnp.bfloat16),
            pltpu.VMEM((rows, peaks), jnp.int32),
            pltpu.VMEM((rows, peaks), jnp.int32),
            pltpu.VMEM((rows, peaks), jnp.bfloat16),
            pltpu.VMEM((CHUNK, peaks), f32),
            pltpu.VMEM((CHUNK, peaks), f32),
            pltpu.VMEM((CHUNK, peaks), f32),
            pltpu.VMEM((HI * GROUP, LANES), f32),
            dma((rows // CHUNK, 3)),
            pltpu.VMEM((rank, rows), f32),
            pltpu.VMEM((rank, width), f32),
            dma((2,)),
        ],
        compiler_params=pltpu.CompilerParams(
            collective_id=0, has_side_effects=True, vmem_limit_bytes=63 * 1024 * 1024
        ),
    )(mass, mobility, weight, basis, profiles)


def solution(mesh):
    pixes, feats = mesh.shape["pix"], mesh.shape["feat"]

    def local(mass_bin, mobility_bin, intensity, basis_init, profile_init):
        basis, profiles = nmf(
            pixes, feats, mass_bin, mobility_bin, intensity, basis_init.T, profile_init
        )
        return (basis.T, profiles)

    return jax.shard_map(
        local,
        mesh=mesh,
        in_specs=(
            P(("pix", "feat"), None),
            P(("pix", "feat"), None),
            P(("pix", "feat"), None),
            P(("pix", "feat"), None),
            P(None, "feat"),
        ),
        out_specs=(P(("pix", "feat"), None), P(None, "feat")),
        check_vma=False,
    )
```

```python
import functools

import jax
import jax.numpy as jnp
from jax import lax
from jax.experimental import pallas as pl
from jax.experimental.pallas import tpu as pltpu
from jax.sharding import PartitionSpec as P

LANES = 128
MZ = 256
MOB = 16
HI = MZ * MOB // LANES
GROUP = 16
UNROLL = 4
CHUNK = 128
ITERS = 2
HALVES = 2
EPS = 1e-06


def bin_peaks(mass_any, mobility_any, weight_any, out_ref, mass_ref, mobility_ref, weight_ref, hi_ref, lo_ref, value_ref, dense_refs, in_sem):
    rows, peaks = mass_any.shape
    hi_iota = lax.broadcasted_iota(jnp.int32, (HI, peaks), 0).astype(jnp.float32).astype(jnp.bfloat16)
    lo_iota = lax.broadcasted_iota(jnp.int32, (LANES, peaks), 0).astype(jnp.float32).astype(jnp.bfloat16)

    def fetches(c):
        own = pl.ds(pl.multiple_of(c * CHUNK, CHUNK), CHUNK)
        pairs = ((mass_any, mass_ref), (mobility_any, mobility_ref), (weight_any, weight_ref))
        return [
            pltpu.make_async_copy(src.at[own], dst.at[own], in_sem.at[c, k])
            for k, (src, dst) in enumerate(pairs)
        ]

    def spread(ref, p, count):
        return jnp.broadcast_to(ref[pl.ds(p, 1), :], (count, peaks)).astype(jnp.bfloat16)

    for c in range(rows // CHUNK):
        for copy in fetches(c):
            copy.start()

    def chunk(c, _):
        for copy in fetches(c):
            copy.wait()
        start = pl.multiple_of(c * CHUNK, CHUNK)
        own = pl.ds(start, CHUNK)
        mass = mass_ref[own, :]
        hi_ref[...] = (mobility_ref[own, :] * (MZ // LANES) + mass // LANES).astype(jnp.float32)
        lo_ref[...] = (mass % LANES).astype(jnp.float32)
        value_ref[...] = weight_ref[own, :].astype(jnp.float32)

        def group(g, _):
            base = pl.multiple_of(g * GROUP * UNROLL, GROUP * UNROLL)
            for u in range(UNROLL):
                for i in range(0, GROUP, 2):
                    left, right = [], []
                    for p in (base + u * GROUP + i, base + u * GROUP + i + 1):
                        left.append(
                            jnp.where(
                                spread(hi_ref, p, HI) == hi_iota, spread(value_ref, p, HI), jnp.bfloat16(0)
                            )
                        )
                        away = spread(lo_ref, p, LANES) - lo_iota
                        right.append(jnp.maximum(jnp.bfloat16(1) - away * away, jnp.bfloat16(0)))
                    both = lax.dot_general(
                        jnp.concatenate(left, 0),
                        jnp.concatenate(right, 0),
                        (((1,), (1,)), ((), ())),
                        preferred_element_type=jnp.float32,
                    )
                    dense_refs[u][pl.ds(i, HI, stride=GROUP), :] = both[:HI, :LANES]
                    dense_refs[u][pl.ds(i + 1, HI, stride=GROUP), :] = both[HI:, LANES:]
                for h in range(HI):
                    out_ref[pl.ds(start + base + u * GROUP, GROUP), h * LANES : (h + 1) * LANES] = dense_refs[u][
                        h * GROUP : (h + 1) * GROUP, :
                    ].astype(jnp.bfloat16)
            return 0

        lax.fori_loop(0, CHUNK // (GROUP * UNROLL), group, 0)
        return 0

    lax.fori_loop(0, rows // CHUNK, chunk, 0)


def nmf_kernel(
    pixes, chips, mass_any, mobility_any, weight_any, basis_any, profiles_any, basis_ref, profiles_ref,
    pair_out, pair_in, gram_out, gram_in, chip_out, chip_in, pix_out, pix_in, whole_ref,
    rounded_ref, gram_h_out, gram_h_in, gram_h_pair_out, gram_h_pair_in, padded_ref,
    pair_sem, gram_sem, chip_sem, pix_sem, whole_sem, block_sem, block_pair_sem, gram_h_sem, gram_h_pair_sem,
    spectra_ref, mass_ref, mobility_ref, weight_ref, hi_ref, lo_ref, value_ref, dense_a, dense_b, dense_c, dense_d, in_sem,
    basis_in, profiles_in, start_sem,
):
    rank, width = profiles_any.shape
    span = width // HALVES
    share = rank // pixes
    pix, feat = lax.axis_index("pix"), lax.axis_index("feat")
    core, chip = lax.rem(feat, 2), feat // 2
    other = 1 - core
    partner = (pix, chip * 2 + other)
    highest = lax.Precision.HIGHEST

    def chip_at(j):
        return lax.rem(chip + j + chips, chips)

    def pix_at(d):
        return lax.rem(pix + d + pixes, pixes)

    barrier = pltpu.get_barrier_semaphore()
    peers = [partner] + [(pix, chip_at(j) * 2 + core) for j in range(1, chips)]
    peers += [(pix_at(d), feat) for d in range(1, pixes)]
    for peer in peers:
        pl.semaphore_signal(barrier, inc=1, device_id=peer, device_id_type=pl.DeviceIdType.MESH)
    starts = [
        pltpu.make_async_copy(basis_any, basis_in, start_sem.at[0]),
        pltpu.make_async_copy(profiles_any, profiles_in, start_sem.at[1]),
    ]
    for copy in starts:
        copy.start()
    bin_peaks(
        mass_any, mobility_any, weight_any, spectra_ref, mass_ref, mobility_ref, weight_ref,
        hi_ref, lo_ref, value_ref, (dense_a, dense_b, dense_c, dense_d), in_sem,
    )
    for copy in starts:
        copy.wait()
    pl.semaphore_wait(barrier, len(peers))

    started = []

    def send(src, dst, sems, device):
        copy = pltpu.make_async_remote_copy(
            src_ref=src, dst_ref=dst, send_sem=sems.at[0], recv_sem=sems.at[1],
            device_id=device, device_id_type=pl.DeviceIdType.MESH,
        )
        copy.start()
        started.append(copy)
        return copy

    def columns(block, half):
        return pl.ds(pl.multiple_of(block * width + half * span, LANES), span)

    def reach(half):
        return pl.ds(0, span if half else span + LANES)

    gram_out[...] = jnp.zeros_like(gram_out)
    gram_h_out[...] = jnp.zeros_like(gram_h_out)
    padded_ref[...] = jnp.zeros_like(padded_ref)
    basis = basis_in[...]
    profiles = [profiles_in[:, half * span : (half + 1) * span] for half in range(HALVES)]
    order = list(range(1, chips)) + [0]
    nt = (((1,), (1,)), ((), ()))
    for step in range(ITERS):
        basis_b = basis.astype(jnp.bfloat16)

        def numer(block, half):
            return jnp.dot(
                basis_b, spectra_ref[:, columns(block, half)], preferred_element_type=jnp.float32
            )

        pair, chip_copy, pix_copy, whole_copy, block_copy, block_pair = {}, {}, {}, {}, {}, {}
        for half in range(HALVES):
            for j in order:
                pair_out[step, half, j] = numer(chip_at(j) * 2 + other, half)
                pair[half, j] = send(
                    pair_out.at[step, half, j], pair_in.at[step, half, j], pair_sem.at[step, half, j], partner
                )
            if half == 0:
                gram_out[step, :, :rank] = lax.dot_general(
                    basis, basis, nt, precision=highest, preferred_element_type=jnp.float32
                )
                gram_copy = send(gram_out.at[step], gram_in.at[step], gram_sem.at[step], partner)
            for j in order:
                mine = numer(chip_at(j) * 2 + core, half)
                if half == 0 and j == order[0]:
                    gram_copy.wait_recv()
                    gram = gram_out[step] + gram_in[step]
                pair[half, j].wait_recv()
                chip_out[step, half, j, :, :span] = mine + pair_in[step, half, j]
                if half == 0:
                    chip_out[step, half, j, :, span:] = gram
                if j:
                    chip_copy[half, j] = send(
                        chip_out.at[step, half, j, :, reach(half)],
                        chip_in.at[step, half, j, :, reach(half)],
                        chip_sem.at[step, half, j],
                        (pix, chip_at(j) * 2 + core),
                    )
        for half in range(HALVES):
            size = span if half else span + LANES
            total = chip_out[step, half, 0, :, :size]
            for j in range(1, chips):
                chip_copy[half, j].wait_recv()
                total = total + chip_in[step, half, j, :, :size]
            if share % 8 == 0:
                pix_out[step, half, :, :, :size] = total.reshape(pixes, share, size)
            else:
                for d in range(pixes):
                    pix_out[step, half, d, :, :size] = total[d * share : (d + 1) * share]
            for d in range(1, pixes):
                pix_copy[half, d] = send(
                    pix_out.at[step, half, pix_at(d), :, reach(half)],
                    pix_in.at[step, half, d, :, reach(half)],
                    pix_sem.at[step, half, d],
                    (pix_at(d), feat),
                )
        for half in range(HALVES):
            size = span if half else span + LANES
            part = pix_out[step, half, pix, :, :size]
            for d in range(1, pixes):
                pix_copy[half, d].wait_recv()
                part = part + pix_in[step, half, d, :, :size]
            whole_ref[step, half, pix, :, :size] = part
            for d in range(1, pixes):
                own = whole_ref.at[step, half, pix, :, reach(half)]
                whole_copy[half, d] = send(own, own, whole_sem.at[step, half, d], (pix_at(d), feat))
        for half in range(HALVES):
            size = span if half else span + LANES
            for d in range(1, pixes):
                whole_copy[half, d].wait_recv()
            if share % 8 == 0:
                whole = whole_ref[step, half, :, :, :size].reshape(rank, size)
            else:
                for d in range(pixes):
                    chip_out[step, half, 0, d * share : (d + 1) * share, :size] = whole_ref[step, half, d, :, :size]
                whole = chip_out[step, half, 0, :, :size]
            if half == 0:
                gram_w = whole[:, span : span + rank]
            profiles[half] = (
                profiles[half]
                * whole[:, :span]
                / (jnp.dot(gram_w, profiles[half], precision=highest, preferred_element_type=jnp.float32) + EPS)
            )
            rounded_ref[step, half, feat] = profiles[half].astype(jnp.bfloat16)
            mine = rounded_ref.at[step, half, feat]
            for j in range(1, chips):
                block_copy[half, j] = send(
                    mine, mine, block_sem.at[step, half, j], (pix, chip_at(j) * 2 + core)
                )
            block_pair[half, 0] = send(mine, mine, block_pair_sem.at[step, half, 0], partner)
            part = lax.dot_general(
                profiles[half], profiles[half], nt, precision=highest, preferred_element_type=jnp.float32
            )
            gram_h = gram_h + part if half else part
        gram_h_out[step, :, :rank] = gram_h
        gram_h_copy = {
            j: send(gram_h_out.at[step], gram_h_in.at[step, j], gram_h_sem.at[step, j], (pix, chip_at(j) * 2 + core))
            for j in range(1, chips)
        }

        def weigh(block, half):
            return lax.dot_general(
                spectra_ref[:, columns(block, half)],
                rounded_ref[step, half, block],
                nt,
                preferred_element_type=jnp.float32,
            )

        numer_w = weigh(feat, 0)
        for half in range(1, HALVES):
            numer_w = numer_w + weigh(feat, half)
        for half in range(HALVES):
            block_pair[half, 0].wait_recv()
            numer_w = numer_w + weigh(chip * 2 + other, half)
        for half in range(HALVES):
            for j in range(1, chips):
                block_copy[half, j].wait_recv()
                came = rounded_ref.at[step, half, chip_at(-j) * 2 + core]
                block_pair[half, j] = send(came, came, block_pair_sem.at[step, half, j], partner)
                numer_w = numer_w + weigh(chip_at(-j) * 2 + core, half)
        gram_h = gram_h_out[step]
        for j in range(1, chips):
            gram_h_copy[j].wait_recv()
            gram_h = gram_h + gram_h_in[step, j]
        gram_h_pair_out[step] = gram_h
        gram_h_pair = send(
            gram_h_pair_out.at[step], gram_h_pair_in.at[step], gram_h_pair_sem.at[step], partner
        )
        for half in range(HALVES):
            for j in range(1, chips):
                block_pair[half, j].wait_recv()
                numer_w = numer_w + weigh(chip_at(-j) * 2 + other, half)
        gram_h_pair.wait_recv()
        gram_h = (gram_h + gram_h_pair_in[step])[:, :rank]
        padded_ref[:, :rank] = numer_w
        basis = (
            basis
            * padded_ref[...].T[:rank, :]
            / (jnp.dot(gram_h, basis, precision=highest, preferred_element_type=jnp.float32) + EPS)
        )
    basis_ref[...] = basis
    for half in range(HALVES):
        profiles_ref[:, half * span : (half + 1) * span] = profiles[half]
    for copy in started:
        copy.wait_send()


def nmf(pixes, feats, mass, mobility, weight, basis, profiles):
    rank, width = profiles.shape
    rows, span = basis.shape[1], width // HALVES
    chips, share = feats // 2, rank // pixes
    f32 = jnp.float32
    peaks = mass.shape[1]
    dma = pltpu.SemaphoreType.DMA
    return pl.pallas_call(
        functools.partial(nmf_kernel, pixes, chips),
        out_shape=[jax.ShapeDtypeStruct(basis.shape, f32), jax.ShapeDtypeStruct(profiles.shape, f32)],
        in_specs=[pl.BlockSpec(memory_space=pltpu.HBM)] * 5,
        out_specs=[pl.BlockSpec(memory_space=pltpu.VMEM)] * 2,
        scratch_shapes=[
            pltpu.VMEM((ITERS, HALVES, chips, rank, span), f32),
            pltpu.VMEM((ITERS, HALVES, chips, rank, span), f32),
            pltpu.VMEM((ITERS, rank, LANES), f32),
            pltpu.VMEM((ITERS, rank, LANES), f32),
            pltpu.VMEM((ITERS, HALVES, chips, rank, span + LANES), f32),
            pltpu.VMEM((ITERS, HALVES, chips, rank, span + LANES), f32),
            pltpu.VMEM((ITERS, HALVES, pixes, share, span + LANES), f32),
            pltpu.VMEM((ITERS, HALVES, pixes, share, span + LANES), f32),
            pltpu.VMEM((ITERS, HALVES, pixes, share, span + LANES), f32),
            pltpu.VMEM((ITERS, HALVES, feats, rank, span), jnp.bfloat16),
            pltpu.VMEM((ITERS, rank, LANES), f32),
            pltpu.VMEM((ITERS, chips, rank, LANES), f32),
            pltpu.VMEM((ITERS, rank, LANES), f32),
            pltpu.VMEM((ITERS, rank, LANES), f32),
            pltpu.VMEM((rows, LANES), f32),
            dma((ITERS, HALVES, chips, 2)),
            dma((ITERS, 2)),
            dma((ITERS, HALVES, chips, 2)),
            dma((ITERS, HALVES, pixes, 2)),
            dma((ITERS, HALVES, pixes, 2)),
            dma((ITERS, HALVES, chips, 2)),
            dma((ITERS, HALVES, chips, 2)),
            dma((ITERS, chips, 2)),
            dma((ITERS, 2)),
            pltpu.VMEM((rows, MZ * MOB), jnp.bfloat16),
            pltpu.VMEM((rows, peaks), jnp.int32),
            pltpu.VMEM((rows, peaks), jnp.int32),
            pltpu.VMEM((rows, peaks), jnp.bfloat16),
            pltpu.VMEM((CHUNK, peaks), f32),
            pltpu.VMEM((CHUNK, peaks), f32),
            pltpu.VMEM((CHUNK, peaks), f32),
            pltpu.VMEM((HI * GROUP, LANES), f32),
            pltpu.VMEM((HI * GROUP, LANES), f32),
            pltpu.VMEM((HI * GROUP, LANES), f32),
            pltpu.VMEM((HI * GROUP, LANES), f32),
            dma((rows // CHUNK, 3)),
            pltpu.VMEM((rank, rows), f32),
            pltpu.VMEM((rank, width), f32),
            dma((2,)),
        ],
        compiler_params=pltpu.CompilerParams(
            collective_id=0, has_side_effects=True, vmem_limit_bytes=63 * 1024 * 1024
        ),
    )(mass, mobility, weight, basis, profiles)


def solution(mesh):
    pixes, feats = mesh.shape["pix"], mesh.shape["feat"]

    def local(mass_bin, mobility_bin, intensity, basis_init, profile_init):
        basis, profiles = nmf(
            pixes, feats, mass_bin, mobility_bin, intensity, basis_init.T, profile_init
        )
        return (basis.T, profiles)

    return jax.shard_map(
        local,
        mesh=mesh,
        in_specs=(
            P(("pix", "feat"), None),
            P(("pix", "feat"), None),
            P(("pix", "feat"), None),
            P(("pix", "feat"), None),
            P(None, "feat"),
        ),
        out_specs=(P(("pix", "feat"), None), P(None, "feat")),
        check_vma=False,
    )
```

```python
import functools

import jax
import jax.numpy as jnp
from jax import lax
from jax.experimental import pallas as pl
from jax.experimental.pallas import tpu as pltpu
from jax.sharding import PartitionSpec as P

LANES = 128
MZ = 256
MOB = 16
HI = MZ * MOB // LANES
GROUP = 16
UNROLL = 4
CHUNK = 128
ITERS = 2
HALVES = 4
EPS = 1e-06


def bin_peaks(mass_any, mobility_any, weight_any, out_ref, mass_ref, mobility_ref, weight_ref, hi_ref, lo_ref, value_ref, dense_refs, in_sem):
    rows, peaks = mass_any.shape
    hi_iota = lax.broadcasted_iota(jnp.int32, (HI, peaks), 0).astype(jnp.float32).astype(jnp.bfloat16)
    lo_iota = lax.broadcasted_iota(jnp.int32, (LANES, peaks), 0).astype(jnp.float32).astype(jnp.bfloat16)

    def fetches(c):
        own = pl.ds(pl.multiple_of(c * CHUNK, CHUNK), CHUNK)
        pairs = ((mass_any, mass_ref), (mobility_any, mobility_ref), (weight_any, weight_ref))
        return [
            pltpu.make_async_copy(src.at[own], dst.at[own], in_sem.at[c, k])
            for k, (src, dst) in enumerate(pairs)
        ]

    def spread(ref, p, count):
        return jnp.broadcast_to(ref[pl.ds(p, 1), :], (count, peaks)).astype(jnp.bfloat16)

    for c in range(rows // CHUNK):
        for copy in fetches(c):
            copy.start()

    def chunk(c, _):
        for copy in fetches(c):
            copy.wait()
        start = pl.multiple_of(c * CHUNK, CHUNK)
        own = pl.ds(start, CHUNK)
        mass = mass_ref[own, :]
        hi_ref[...] = (mobility_ref[own, :] * (MZ // LANES) + mass // LANES).astype(jnp.float32)
        lo_ref[...] = (mass % LANES).astype(jnp.float32)
        value_ref[...] = weight_ref[own, :].astype(jnp.float32)

        def group(g, _):
            base = pl.multiple_of(g * GROUP * UNROLL, GROUP * UNROLL)
            for u in range(UNROLL):
                for i in range(0, GROUP, 2):
                    left, right = [], []
                    for p in (base + u * GROUP + i, base + u * GROUP + i + 1):
                        left.append(
                            jnp.where(
                                spread(hi_ref, p, HI) == hi_iota, spread(value_ref, p, HI), jnp.bfloat16(0)
                            )
                        )
                        away = spread(lo_ref, p, LANES) - lo_iota
                        right.append(jnp.maximum(jnp.bfloat16(1) - away * away, jnp.bfloat16(0)))
                    both = lax.dot_general(
                        jnp.concatenate(left, 0),
                        jnp.concatenate(right, 0),
                        (((1,), (1,)), ((), ())),
                        preferred_element_type=jnp.float32,
                    )
                    dense_refs[u][pl.ds(i, HI, stride=GROUP), :] = both[:HI, :LANES]
                    dense_refs[u][pl.ds(i + 1, HI, stride=GROUP), :] = both[HI:, LANES:]
                for h in range(HI):
                    out_ref[pl.ds(start + base + u * GROUP, GROUP), h * LANES : (h + 1) * LANES] = dense_refs[u][
                        h * GROUP : (h + 1) * GROUP, :
                    ].astype(jnp.bfloat16)
            return 0

        lax.fori_loop(0, CHUNK // (GROUP * UNROLL), group, 0)
        return 0

    lax.fori_loop(0, rows // CHUNK, chunk, 0)


def nmf_kernel(
    pixes, chips, mass_any, mobility_any, weight_any, basis_any, profiles_any, basis_ref, profiles_ref,
    pair_out, pair_in, gram_out, gram_in, chip_out, chip_in, pix_out, pix_in, whole_ref,
    rounded_ref, gram_h_out, gram_h_in, gram_h_pair_out, gram_h_pair_in, padded_ref,
    pair_sem, gram_sem, chip_sem, pix_sem, whole_sem, block_sem, block_pair_sem, gram_h_sem, gram_h_pair_sem,
    spectra_ref, mass_ref, mobility_ref, weight_ref, hi_ref, lo_ref, value_ref, dense_a, dense_b, dense_c, dense_d, in_sem,
    basis_in, profiles_in, start_sem,
):
    rank, width = profiles_any.shape
    span = width // HALVES
    share = rank // pixes
    pix, feat = lax.axis_index("pix"), lax.axis_index("feat")
    core, chip = lax.rem(feat, 2), feat // 2
    other = 1 - core
    partner = (pix, chip * 2 + other)
    highest = lax.Precision.HIGHEST

    def chip_at(j):
        return lax.rem(chip + j + chips, chips)

    def pix_at(d):
        return lax.rem(pix + d + pixes, pixes)

    barrier = pltpu.get_barrier_semaphore()
    peers = [partner] + [(pix, chip_at(j) * 2 + core) for j in range(1, chips)]
    peers += [(pix_at(d), feat) for d in range(1, pixes)]
    for peer in peers:
        pl.semaphore_signal(barrier, inc=1, device_id=peer, device_id_type=pl.DeviceIdType.MESH)
    starts = [
        pltpu.make_async_copy(basis_any, basis_in, start_sem.at[0]),
        pltpu.make_async_copy(profiles_any, profiles_in, start_sem.at[1]),
    ]
    for copy in starts:
        copy.start()
    bin_peaks(
        mass_any, mobility_any, weight_any, spectra_ref, mass_ref, mobility_ref, weight_ref,
        hi_ref, lo_ref, value_ref, (dense_a, dense_b, dense_c, dense_d), in_sem,
    )
    for copy in starts:
        copy.wait()
    pl.semaphore_wait(barrier, len(peers))

    started = []

    def send(src, dst, sems, device):
        copy = pltpu.make_async_remote_copy(
            src_ref=src, dst_ref=dst, send_sem=sems.at[0], recv_sem=sems.at[1],
            device_id=device, device_id_type=pl.DeviceIdType.MESH,
        )
        copy.start()
        started.append(copy)
        return copy

    def columns(block, half):
        return pl.ds(pl.multiple_of(block * width + half * span, LANES), span)

    def reach(half):
        return pl.ds(0, span if half else span + LANES)

    gram_out[...] = jnp.zeros_like(gram_out)
    gram_h_out[...] = jnp.zeros_like(gram_h_out)
    padded_ref[...] = jnp.zeros_like(padded_ref)
    basis = basis_in[...]
    profiles = [profiles_in[:, half * span : (half + 1) * span] for half in range(HALVES)]
    order = list(range(1, chips)) + [0]
    nt = (((1,), (1,)), ((), ()))
    for step in range(ITERS):
        basis_b = basis.astype(jnp.bfloat16)

        def numer(block, half):
            return jnp.dot(
                basis_b, spectra_ref[:, columns(block, half)], preferred_element_type=jnp.float32
            )

        pair, chip_copy, pix_copy, whole_copy, block_copy, block_pair = {}, {}, {}, {}, {}, {}
        for half in range(HALVES):
            for j in order:
                pair_out[step, half, j] = numer(chip_at(j) * 2 + other, half)
                pair[half, j] = send(
                    pair_out.at[step, half, j], pair_in.at[step, half, j], pair_sem.at[step, half, j], partner
                )
            if half == 0:
                gram_out[step, :, :rank] = lax.dot_general(
                    basis, basis, nt, precision=highest, preferred_element_type=jnp.float32
                )
                gram_copy = send(gram_out.at[step], gram_in.at[step], gram_sem.at[step], partner)
            for j in order:
                mine = numer(chip_at(j) * 2 + core, half)
                if half == 0 and j == order[0]:
                    gram_copy.wait_recv()
                    gram = gram_out[step] + gram_in[step]
                pair[half, j].wait_recv()
                chip_out[step, half, j, :, :span] = mine + pair_in[step, half, j]
                if half == 0:
                    chip_out[step, half, j, :, span:] = gram
                if j:
                    chip_copy[half, j] = send(
                        chip_out.at[step, half, j, :, reach(half)],
                        chip_in.at[step, half, j, :, reach(half)],
                        chip_sem.at[step, half, j],
                        (pix, chip_at(j) * 2 + core),
                    )
        for half in range(HALVES):
            size = span if half else span + LANES
            total = chip_out[step, half, 0, :, :size]
            for j in range(1, chips):
                chip_copy[half, j].wait_recv()
                total = total + chip_in[step, half, j, :, :size]
            if share % 8 == 0:
                pix_out[step, half, :, :, :size] = total.reshape(pixes, share, size)
            else:
                for d in range(pixes):
                    pix_out[step, half, d, :, :size] = total[d * share : (d + 1) * share]
            for d in range(1, pixes):
                pix_copy[half, d] = send(
                    pix_out.at[step, half, pix_at(d), :, reach(half)],
                    pix_in.at[step, half, d, :, reach(half)],
                    pix_sem.at[step, half, d],
                    (pix_at(d), feat),
                )
        for half in range(HALVES):
            size = span if half else span + LANES
            part = pix_out[step, half, pix, :, :size]
            for d in range(1, pixes):
                pix_copy[half, d].wait_recv()
                part = part + pix_in[step, half, d, :, :size]
            whole_ref[step, half, pix, :, :size] = part
            for d in range(1, pixes):
                own = whole_ref.at[step, half, pix, :, reach(half)]
                whole_copy[half, d] = send(own, own, whole_sem.at[step, half, d], (pix_at(d), feat))
        for half in range(HALVES):
            size = span if half else span + LANES
            for d in range(1, pixes):
                whole_copy[half, d].wait_recv()
            if share % 8 == 0:
                whole = whole_ref[step, half, :, :, :size].reshape(rank, size)
            else:
                for d in range(pixes):
                    chip_out[step, half, 0, d * share : (d + 1) * share, :size] = whole_ref[step, half, d, :, :size]
                whole = chip_out[step, half, 0, :, :size]
            if half == 0:
                gram_w = whole[:, span : span + rank]
            profiles[half] = (
                profiles[half]
                * whole[:, :span]
                / (jnp.dot(gram_w, profiles[half], precision=highest, preferred_element_type=jnp.float32) + EPS)
            )
            rounded_ref[step, half, feat] = profiles[half].astype(jnp.bfloat16)
            mine = rounded_ref.at[step, half, feat]
            for j in range(1, chips):
                block_copy[half, j] = send(
                    mine, mine, block_sem.at[step, half, j], (pix, chip_at(j) * 2 + core)
                )
            block_pair[half, 0] = send(mine, mine, block_pair_sem.at[step, half, 0], partner)
            part = lax.dot_general(
                profiles[half], profiles[half], nt, precision=highest, preferred_element_type=jnp.float32
            )
            gram_h = gram_h + part if half else part
        gram_h_out[step, :, :rank] = gram_h
        gram_h_copy = {
            j: send(gram_h_out.at[step], gram_h_in.at[step, j], gram_h_sem.at[step, j], (pix, chip_at(j) * 2 + core))
            for j in range(1, chips)
        }

        def weigh(block, half):
            return lax.dot_general(
                spectra_ref[:, columns(block, half)],
                rounded_ref[step, half, block],
                nt,
                preferred_element_type=jnp.float32,
            )

        numer_w = weigh(feat, 0)
        for half in range(1, HALVES):
            numer_w = numer_w + weigh(feat, half)
        for half in range(HALVES):
            block_pair[half, 0].wait_recv()
            numer_w = numer_w + weigh(chip * 2 + other, half)
        for half in range(HALVES):
            for j in range(1, chips):
                block_copy[half, j].wait_recv()
                came = rounded_ref.at[step, half, chip_at(-j) * 2 + core]
                block_pair[half, j] = send(came, came, block_pair_sem.at[step, half, j], partner)
                numer_w = numer_w + weigh(chip_at(-j) * 2 + core, half)
        gram_h = gram_h_out[step]
        for j in range(1, chips):
            gram_h_copy[j].wait_recv()
            gram_h = gram_h + gram_h_in[step, j]
        gram_h_pair_out[step] = gram_h
        gram_h_pair = send(
            gram_h_pair_out.at[step], gram_h_pair_in.at[step], gram_h_pair_sem.at[step], partner
        )
        for half in range(HALVES):
            for j in range(1, chips):
                block_pair[half, j].wait_recv()
                numer_w = numer_w + weigh(chip_at(-j) * 2 + other, half)
        gram_h_pair.wait_recv()
        gram_h = (gram_h + gram_h_pair_in[step])[:, :rank]
        padded_ref[:, :rank] = numer_w
        basis = (
            basis
            * padded_ref[...].T[:rank, :]
            / (jnp.dot(gram_h, basis, precision=highest, preferred_element_type=jnp.float32) + EPS)
        )
    basis_ref[...] = basis
    for half in range(HALVES):
        profiles_ref[:, half * span : (half + 1) * span] = profiles[half]
    for copy in started:
        copy.wait_send()


def nmf(pixes, feats, mass, mobility, weight, basis, profiles):
    rank, width = profiles.shape
    rows, span = basis.shape[1], width // HALVES
    chips, share = feats // 2, rank // pixes
    f32 = jnp.float32
    peaks = mass.shape[1]
    dma = pltpu.SemaphoreType.DMA
    return pl.pallas_call(
        functools.partial(nmf_kernel, pixes, chips),
        out_shape=[jax.ShapeDtypeStruct(basis.shape, f32), jax.ShapeDtypeStruct(profiles.shape, f32)],
        in_specs=[pl.BlockSpec(memory_space=pltpu.HBM)] * 5,
        out_specs=[pl.BlockSpec(memory_space=pltpu.VMEM)] * 2,
        scratch_shapes=[
            pltpu.VMEM((ITERS, HALVES, chips, rank, span), f32),
            pltpu.VMEM((ITERS, HALVES, chips, rank, span), f32),
            pltpu.VMEM((ITERS, rank, LANES), f32),
            pltpu.VMEM((ITERS, rank, LANES), f32),
            pltpu.VMEM((ITERS, HALVES, chips, rank, span + LANES), f32),
            pltpu.VMEM((ITERS, HALVES, chips, rank, span + LANES), f32),
            pltpu.VMEM((ITERS, HALVES, pixes, share, span + LANES), f32),
            pltpu.VMEM((ITERS, HALVES, pixes, share, span + LANES), f32),
            pltpu.VMEM((ITERS, HALVES, pixes, share, span + LANES), f32),
            pltpu.VMEM((ITERS, HALVES, feats, rank, span), jnp.bfloat16),
            pltpu.VMEM((ITERS, rank, LANES), f32),
            pltpu.VMEM((ITERS, chips, rank, LANES), f32),
            pltpu.VMEM((ITERS, rank, LANES), f32),
            pltpu.VMEM((ITERS, rank, LANES), f32),
            pltpu.VMEM((rows, LANES), f32),
            dma((ITERS, HALVES, chips, 2)),
            dma((ITERS, 2)),
            dma((ITERS, HALVES, chips, 2)),
            dma((ITERS, HALVES, pixes, 2)),
            dma((ITERS, HALVES, pixes, 2)),
            dma((ITERS, HALVES, chips, 2)),
            dma((ITERS, HALVES, chips, 2)),
            dma((ITERS, chips, 2)),
            dma((ITERS, 2)),
            pltpu.VMEM((rows, MZ * MOB), jnp.bfloat16),
            pltpu.VMEM((rows, peaks), jnp.int32),
            pltpu.VMEM((rows, peaks), jnp.int32),
            pltpu.VMEM((rows, peaks), jnp.bfloat16),
            pltpu.VMEM((CHUNK, peaks), f32),
            pltpu.VMEM((CHUNK, peaks), f32),
            pltpu.VMEM((CHUNK, peaks), f32),
            pltpu.VMEM((HI * GROUP, LANES), f32),
            pltpu.VMEM((HI * GROUP, LANES), f32),
            pltpu.VMEM((HI * GROUP, LANES), f32),
            pltpu.VMEM((HI * GROUP, LANES), f32),
            dma((rows // CHUNK, 3)),
            pltpu.VMEM((rank, rows), f32),
            pltpu.VMEM((rank, width), f32),
            dma((2,)),
        ],
        compiler_params=pltpu.CompilerParams(
            collective_id=0, has_side_effects=True, vmem_limit_bytes=63 * 1024 * 1024
        ),
    )(mass, mobility, weight, basis, profiles)


def solution(mesh):
    pixes, feats = mesh.shape["pix"], mesh.shape["feat"]

    def local(mass_bin, mobility_bin, intensity, basis_init, profile_init):
        basis, profiles = nmf(
            pixes, feats, mass_bin, mobility_bin, intensity, basis_init.T, profile_init
        )
        return (basis.T, profiles)

    return jax.shard_map(
        local,
        mesh=mesh,
        in_specs=(
            P(("pix", "feat"), None),
            P(("pix", "feat"), None),
            P(("pix", "feat"), None),
            P(("pix", "feat"), None),
            P(None, "feat"),
        ),
        out_specs=(P(("pix", "feat"), None), P(None, "feat")),
        check_vma=False,
    )
```
